512 devices in a mesh: seq: 64 (over y, z), head: 8 (over x, core).
Axes of the slice: x: 4, y: 4, z: 16, core: 2. Of those that a mesh axis runs over, the one named last changes fastest.
Arguments:
- mixer_input: bfloat16 [16384, 8192], P('seq', 'head'), may hold values from -6 to 6
- gate_input: bfloat16 [16384, 8192], P('seq', 'head'), may hold values from -5 to 8
- input_map: bfloat16 [16384, 1024], P('seq', 'head'), may hold values from -0.5390625 to 0.5390625
- output_map: bfloat16 [16384, 1024], P('seq', 'head'), may hold values from -0.5390625 to 0.5390625
- step_size: float32 [128, 16384], P('head', 'seq'), may hold values from 0.0125 to 5000, as said below
- decay_rate: float32 [128], P('head'), may hold values from 1e-05 to 0.05
- skip_gain: float32 [128], P('head'), may hold values from 0.2 to 2
- norm_gain: float32 [8192], P('head'), may hold values from 0.25 to 1.75
- queries: bfloat16 [16384, 8192], P('seq', 'head'), may hold values from -200 to 200
- key_rows: bfloat16 [16384, 1024], P('seq', 'head'), may hold values from -6 to 6
- values: bfloat16 [16384, 1024], P('seq', 'head'), may hold values from -6 to 6
- segment: int32 [16384], P('seq'), may hold values from 0 to 15, never falling along the last dimension, each value on 1 to 2048 neighbouring positions
Outputs:
- state_output: bfloat16 [16384, 8192], P('seq', 'head')
- attention_output: bfloat16 [16384, 8192], P('seq', 'head')
The draws below stay inside these ranges and needn't reach their ends.
Inputs may be any that keep to these rules, and one draw needn't show every extreme that they name: `segment`: segment numbers never fall along the sequence; each document has 1 to 2048 tokens and some document has exactly 2048. `step_size`: positive steps.
All inputs are finite; a program needn't handle non-finite values.
Results may differ from the reference program's by a relative error of at most 0.011.
Values may be sent and summed in bfloat16 or wider, within the bound.
A program may use at most 128 MiB of HBM per device.

```python
import math
from functools import partial
import jax
import jax.numpy as jnp
import numpy as np
from jax import lax

SSD_HEADS = 128
HEAD_P = 64
STATE_N = 128
GROUPS = 8
ATT_HEADS = 64
KV_HEADS = 8
HEAD_D = 128
TOKENS_PER_SHARD = 256
DOC_SPAN = 8
SEQUENCE_TOKENS = 16384
DOC_MOST = 2048
DOCS = 16
N_SEQ = 64


def attention_pair(key):
    base = jax.random.fold_in(key, 4242)
    seed_query, seed_keys = jax.random.split(base, 2)
    repeat_count = ATT_HEADS // KV_HEADS
    query_draw = jnp.clip(jax.random.normal(seed_query, (SEQUENCE_TOKENS, KV_HEADS, repeat_count, HEAD_D), jnp.float32), -6.0, 6.0)
    key_draw = jnp.clip(jax.random.normal(seed_keys, (SEQUENCE_TOKENS, KV_HEADS, HEAD_D), jnp.float32), -6.0, 6.0)
    return (query_draw.reshape(SEQUENCE_TOKENS, ATT_HEADS * HEAD_D), key_draw.reshape(SEQUENCE_TOKENS, KV_HEADS * HEAD_D))


def draw_queries(key, part):
    return attention_pair(key)[0].astype(jnp.bfloat16)


def draw_key_rows(key, part):
    return attention_pair(key)[1].astype(jnp.bfloat16)


def draw_step_size(key, part):
    jitter_seed, floor_seed, spike_seed, peak_seed = jax.random.split(jax.random.fold_in(key, 11), 4)
    rough = jnp.exp(jax.random.uniform(jitter_seed, (SSD_HEADS, SEQUENCE_TOKENS), jnp.float32, -0.693, 0.693))
    block_count = SEQUENCE_TOKENS // TOKENS_PER_SHARD
    level = jnp.exp(jax.random.uniform(floor_seed, (1, block_count), jnp.float32, -0.693, 0.693))
    level = jnp.repeat(level, TOKENS_PER_SHARD, axis=1)
    spike_amount = jax.random.randint(spike_seed, (1, SEQUENCE_TOKENS), 0, 2 * TOKENS_PER_SHARD) == 0
    peak_value = jax.random.uniform(peak_seed, (1, SEQUENCE_TOKENS), jnp.float32, 1000.0, 5000.0)
    sampled_step = rough * level
    return jnp.where(spike_amount, peak_value, sampled_step)


def draw_gate_input(key, part):
    noise = jnp.clip(jax.random.normal(jax.random.fold_in(key, 31), (SEQUENCE_TOKENS, SSD_HEADS * HEAD_P), jnp.float32), -5.0, 5.0)
    ramp = (jnp.arange(SSD_HEADS * HEAD_P) // HEAD_P).astype(jnp.float32) / (SSD_HEADS - 1)
    return (noise + 1.5 * ramp[None, :]).astype(jnp.bfloat16)


def steps_of(key, dims, pieces, least, high):
    def one(axis_at, parts):
        draws = jax.random.uniform(jax.random.fold_in(jax.random.fold_in(key, 6), axis_at), (parts,), jnp.float32, least / len(pieces), high / len(pieces))
        return jnp.repeat(jnp.exp(draws), dims[axis_at] // parts).reshape((-1,) + (1,) * (len(dims) - axis_at - 1))

    gain = one(*pieces[0])
    for cut in pieces[1:]:
        gain = gain * one(*cut)
    return gain


def profile(amount, total, limit, skew):
    weights = [(1 << 20) // math.isqrt(rank ** skew) + 1 for rank in range(2, amount + 1)]
    surplus, holding = total - limit - (amount - 1), [1] * (amount - 1)
    while surplus > 0:
        candidates = [i for i in range(amount - 1) if holding[i] < limit]
        mass, budget = sum([weights[i] for i in candidates]), surplus
        for i in candidates:
            extra = min(limit - holding[i], max(1, budget * weights[i] // mass), surplus)
            holding[i] = holding[i] + extra
            surplus = surplus - extra
    return np.array([limit] + holding)


def ragged(key, number_of, total, most, slope):
    if number_of == 2:
        one = jax.random.randint(key, (), max(1, total - most), min(most, total - 1) + 1)
        return jnp.stack([one, total - one])
    tallies = jnp.asarray(profile(number_of, total, most, slope), jnp.int32)
    couples = (number_of - 1) // 2
    donor, sink = tallies[1:1 + 2 * couples:2], tallies[2:2 + 2 * couples:2]
    room = jnp.minimum(donor - 1, most - sink)
    shifted = jax.random.randint(jax.random.fold_in(key, 1), (couples,), 0, 1 << 20) % (room + 1)
    tallies = tallies.at[1:1 + 2 * couples:2].set(donor - shifted).at[2:2 + 2 * couples:2].set(sink + shifted)
    return tallies[jax.random.permutation(jax.random.fold_in(key, 2), number_of)]


def normal_values(stream_key, dims, deviation, bound, cuts=(), kind=jnp.bfloat16):
    gain = steps_of(stream_key, dims, cuts, -0.22, 0.18) if cuts else 1.0
    drawn = jax.random.normal(stream_key, dims, jnp.float32) * deviation * gain
    return jnp.minimum(jnp.maximum(drawn, -bound), bound).astype(kind)


def setup_inputs(seed: int = 0) -> dict:
    seeds = jax.random.split(jax.random.key(seed), 13)
    return {
        "mixer_input": normal_values(seeds[0], (SEQUENCE_TOKENS, SSD_HEADS * HEAD_P), 1.0, 6.0, ((0, 64), (1, 8))),
        "gate_input": draw_gate_input(jax.random.fold_in(seeds[12], 71), 0),
        "input_map": normal_values(seeds[2], (SEQUENCE_TOKENS, GROUPS * STATE_N), 0.09, 0.5390625, ((0, 64), (1, 8))),
        "output_map": normal_values(seeds[3], (SEQUENCE_TOKENS, GROUPS * STATE_N), 0.09, 0.5390625, ((0, 64), (1, 8))),
        "step_size": draw_step_size(jax.random.fold_in(seeds[12], 71), 0),
        "decay_rate": jnp.clip(jnp.exp(math.log(0.05) - 8.517193 * jax.random.uniform(seeds[5], (SSD_HEADS,), jnp.float32) ** steps_of(seeds[5], (SSD_HEADS,), ((0, 8),), -0.2, 0.2)), 9.999999747378752e-06, 0.05),
        "skip_gain": jnp.clip(0.2 + 1.8 * jax.random.uniform(seeds[6], (SSD_HEADS,), jnp.float32) ** steps_of(seeds[6], (SSD_HEADS,), ((0, 8),), -0.2, 0.2), 0.2, 2.0),
        "norm_gain": jnp.clip(1.0 + 0.15 * jax.random.normal(seeds[7], (SSD_HEADS * HEAD_P,), jnp.float32), 0.25, 1.75),
        "queries": draw_queries(jax.random.fold_in(seeds[12], 71), 0),
        "key_rows": draw_key_rows(jax.random.fold_in(seeds[12], 71), 0),
        "values": normal_values(seeds[10], (SEQUENCE_TOKENS, KV_HEADS * HEAD_D), 1.0, 6.0, ((0, 64), (1, 8))),
        "segment": jnp.searchsorted(jnp.cumsum(ragged(seeds[11], DOCS, SEQUENCE_TOKENS, DOC_MOST, 1)), jnp.arange(SEQUENCE_TOKENS), side="right").astype(jnp.int32),
    }


def mixer_step(carried, inputs, decay_rate, skip_gain, norm_gain):
    state_in, doc_tag = carried
    block_input, block_gate, block_in_map, block_out_map, block_step, block_segment = inputs
    row_count = block_input.shape[0]
    head_count = block_step.shape[0]
    group_count = block_in_map.shape[1] // STATE_N
    repeat_count = head_count // group_count
    mixer_heads = block_input.astype(jnp.float32).reshape(row_count, head_count, HEAD_P).transpose(1, 0, 2)
    in_heads = jnp.repeat(block_in_map.astype(jnp.float32).reshape(row_count, group_count, STATE_N).transpose(1, 0, 2), repeat_count, axis=0)
    out_heads = jnp.repeat(block_out_map.astype(jnp.float32).reshape(row_count, group_count, STATE_N).transpose(1, 0, 2), repeat_count, axis=0)
    seg_float = block_segment.astype(jnp.float32)
    cumulative = jnp.cumsum(block_step * decay_rate[:, None], axis=1)
    position = jnp.arange(row_count, dtype=jnp.int32)
    allowed = (block_segment[:, None] == block_segment[None, :]) & (position[None, :] <= position[:, None])
    spread_gap = cumulative[:, :, None] - cumulative[:, None, :]
    decay_grid = jnp.where(allowed[None], jnp.exp(-jnp.where(allowed[None], spread_gap, 0.0)), 0.0)
    inner_head = jnp.einsum('htn,hsn->hts', out_heads, in_heads)
    mixing = (decay_grid * inner_head).astype(jnp.bfloat16)
    mixing = lax.optimization_barrier(mixing).astype(jnp.float32)
    intra = jnp.einsum('hts,hsp->htp', mixing, mixer_heads)
    last_cum = cumulative[:, -1]
    tail = jnp.where(block_segment[None, :] == block_segment[-1], jnp.exp(-(last_cum[:, None] - cumulative)), 0.0)
    scaled = (tail[:, :, None] * in_heads).astype(jnp.bfloat16)
    scaled = lax.optimization_barrier(scaled).astype(jnp.float32)
    block_state = jnp.einsum('hsp,hsn->hpn', mixer_heads, scaled)
    enter = jnp.where(seg_float[None, :] == doc_tag, jnp.exp(-cumulative), 0.0)
    incoming = jnp.einsum('htn,hpn->htp', out_heads, state_in, precision=lax.Precision.HIGHEST)
    mixed = intra + enter[:, :, None] * incoming + skip_gain[:, None, None] * mixer_heads
    gate_heads = block_gate.astype(jnp.float32).reshape(row_count, head_count, HEAD_P).transpose(1, 0, 2)
    gated = mixed * jax.nn.silu(gate_heads)
    mean_square = lax.optimization_barrier(jnp.sum(gated * gated, axis=(0, 2))) / (SSD_HEADS * HEAD_P)
    normed = gated * lax.rsqrt(mean_square + 1e-05)[None, :, None] * norm_gain.reshape(head_count, 1, HEAD_P)
    block_output = normed.transpose(1, 0, 2).reshape(row_count, head_count * HEAD_P).astype(jnp.bfloat16)
    total_decay = jnp.exp(-last_cum) * (block_segment[0] == block_segment[-1]).astype(jnp.float32)
    joined = (seg_float[0] == doc_tag).astype(jnp.float32)
    next_state = (total_decay * joined)[:, None, None] * state_in + block_state
    return ((next_state, seg_float[-1]), block_output)

def attention_block(block_index, queries, key_pad, value_pad, segment, segment_pad):
    repeat_count = ATT_HEADS // KV_HEADS
    span_rows = (DOC_SPAN + 1) * TOKENS_PER_SHARD
    start = block_index * TOKENS_PER_SHARD
    query_block = lax.dynamic_slice_in_dim(queries, start, TOKENS_PER_SHARD, 0).astype(jnp.float32).reshape(TOKENS_PER_SHARD, KV_HEADS, repeat_count, HEAD_D)
    key_block = lax.dynamic_slice_in_dim(key_pad, start, span_rows, 0).astype(jnp.float32).reshape(span_rows, KV_HEADS, HEAD_D)
    value_block = lax.dynamic_slice_in_dim(value_pad, start, span_rows, 0).astype(jnp.float32).reshape(span_rows, KV_HEADS, HEAD_D)
    query_seg = lax.dynamic_slice_in_dim(segment, start, TOKENS_PER_SHARD, 0)
    key_seg = lax.dynamic_slice_in_dim(segment_pad, start, span_rows, 0)
    query_pos = start + jnp.arange(TOKENS_PER_SHARD, dtype=jnp.int32)
    key_pos = start - DOC_SPAN * TOKENS_PER_SHARD + jnp.arange(span_rows, dtype=jnp.int32)
    allowed = (key_pos[None, :] <= query_pos[:, None]) & (key_seg[None, :] == query_seg[:, None])
    scores = jnp.einsum('tkrd,ukd->krtu', query_block, key_block) * (1.0 / math.sqrt(HEAD_D))
    scores = jnp.where(allowed[None, None], scores, -jnp.inf)
    row_best = lax.optimization_barrier(jnp.max(scores, axis=3, keepdims=True))
    weights = jnp.exp(scores - row_best)
    row_total = lax.optimization_barrier(jnp.sum(weights, axis=3))
    rounded = lax.optimization_barrier(weights.astype(jnp.bfloat16)).astype(jnp.float32)
    summed = jnp.einsum('krtu,ukd->krtd', rounded, value_block) / row_total[..., None]
    return summed.transpose(2, 0, 1, 3).reshape(TOKENS_PER_SHARD, ATT_HEADS * HEAD_D).astype(jnp.bfloat16)

def reference(mixer_input, gate_input, input_map, output_map, step_size, decay_rate, skip_gain, norm_gain, queries, key_rows, values, segment):
    inputs = (mixer_input.reshape(N_SEQ, TOKENS_PER_SHARD, SSD_HEADS * HEAD_P), gate_input.reshape(N_SEQ, TOKENS_PER_SHARD, SSD_HEADS * HEAD_P), input_map.reshape(N_SEQ, TOKENS_PER_SHARD, GROUPS * STATE_N), output_map.reshape(N_SEQ, TOKENS_PER_SHARD, GROUPS * STATE_N), step_size.reshape(SSD_HEADS, N_SEQ, TOKENS_PER_SHARD).transpose(1, 0, 2), segment.reshape(N_SEQ, TOKENS_PER_SHARD))
    initial = (jnp.zeros((SSD_HEADS, HEAD_P, STATE_N), jnp.float32), jnp.array(-1.0, jnp.float32))
    stepper = partial(mixer_step, decay_rate=decay_rate, skip_gain=skip_gain, norm_gain=norm_gain)
    finished, blocks_out = lax.scan(stepper, initial, inputs)
    state_output = blocks_out.reshape(SEQUENCE_TOKENS, SSD_HEADS * HEAD_P)
    front = DOC_SPAN * TOKENS_PER_SHARD
    key_pad = jnp.pad(key_rows, ((front, 0), (0, 0)))
    value_pad = jnp.pad(values, ((front, 0), (0, 0)))
    segment_pad = jnp.pad(segment, (front, 0), constant_values=-1)
    attended = lax.map(lambda index: attention_block(index, queries, key_pad, value_pad, segment, segment_pad), jnp.arange(N_SEQ, dtype=jnp.int32))
    attention_output = attended.reshape(SEQUENCE_TOKENS, ATT_HEADS * HEAD_D)
    return (state_output, attention_output)
```

```python
import math

import jax
import jax.numpy as jnp
from jax import lax
from jax.experimental import pallas as pl
from jax.experimental.pallas import tpu as pltpu
from jax.sharding import PartitionSpec as P

SSD_HEADS = 128
HEAD_P = 64
STATE_N = 128
ATT_HEADS = 64
HEAD_D = 128
DOC_SPAN = 8
TOKENS = 256
N_SEQ = 64
RING = 16
N_HEAD = 8
LOCAL_HEADS = SSD_HEADS // N_HEAD
LOCAL_ATT = ATT_HEADS // N_HEAD
PAIRS = LOCAL_HEADS // 2
KT_ROWS = HEAD_D + 16
MSG = HEAD_P + 16
LOG2E = 1.0 / math.log(2.0)
SCORE_SCALE = LOG2E / math.sqrt(HEAD_D)
FAR = float(2**19)
MESH = pl.DeviceIdType.MESH
F32 = jnp.float32
BF16 = jnp.bfloat16


def dot(a, b, contract=((1,), (0,))):
    return lax.dot_general(a, b, (contract, ((), ())), preferred_element_type=F32)


def kernel(
    x_ref, gate_ref, in_ref, out_ref, step_ref, decay_ref, skip_ref, gain_ref, q_ref, k_ref, v_ref, seg_ref,
    state_ref, att_ref,
    kt_buf, v_buf, send_buf, scan_buf, local_buf, back_buf, carry_buf, in_buf, sq_buf,
    y_buf, acc_buf, max_buf, g_buf, onehot_buf, col_buf, cum_buf,
    kt_send, kt_recv, v_send, v_recv, a_send, a_recv, c_send, c_recv, b_send, b_recv, s_send, s_recv,
):
    me = lax.axis_index("seq")
    head = lax.axis_index("head")
    row, z = me // RING, me % RING
    succ, pred = (me + 1) % N_SEQ, (me + N_SEQ - 1) % N_SEQ
    below, above = (me + RING) % N_SEQ, (me + N_SEQ - RING) % N_SEQ

    def ring(d):
        return row * RING + (z + d) % RING

    barrier = pltpu.get_barrier_semaphore()
    for d in sorted(range(1, RING), key=lambda d: -min(d, RING - d)):
        pl.semaphore_signal(barrier, inc=1, device_id={"seq": ring(d)}, device_id_type=MESH)
    for other in (below, above, succ, pred):
        pl.semaphore_signal(barrier, inc=1, device_id={"seq": other}, device_id_type=MESH)
    for d in range(1, N_HEAD):
        pl.semaphore_signal(barrier, inc=1, device_id={"head": (head + d) % N_HEAD}, device_id_type=MESH)

    def kv_copies(hop):
        return (
            pltpu.make_async_remote_copy(
                src_ref=kt_buf.at[hop, pl.ds(0, KT_ROWS)],
                dst_ref=kt_buf.at[hop + 1, pl.ds(0, KT_ROWS)],
                send_sem=kt_send.at[hop],
                recv_sem=kt_recv.at[hop],
                device_id={"seq": succ},
                device_id_type=MESH,
            ),
            pltpu.make_async_remote_copy(
                src_ref=v_buf.at[hop],
                dst_ref=v_buf.at[hop + 1],
                send_sem=v_send.at[hop],
                recv_sem=v_recv.at[hop],
                device_id={"seq": succ},
                device_id_type=MESH,
            ),
        )

    def scan_copy(d):
        return pltpu.make_async_remote_copy(
            src_ref=send_buf.at[(z + d) % RING],
            dst_ref=scan_buf.at[z],
            send_sem=a_send.at[d],
            recv_sem=a_recv.at[d],
            device_id={"seq": ring(d)},
            device_id_type=MESH,
        )

    def back_copy(d):
        return pltpu.make_async_remote_copy(
            src_ref=back_buf.at[(z + d) % RING],
            dst_ref=in_buf.at[z],
            send_sem=b_send.at[d],
            recv_sem=b_recv.at[d],
            device_id={"seq": ring(d)},
            device_id_type=MESH,
        )

    def square_copy(d):
        return pltpu.make_async_remote_copy(
            src_ref=sq_buf.at[head],
            dst_ref=sq_buf.at[head],
            send_sem=s_send.at[d],
            recv_sem=s_recv.at[d],
            device_id={"head": (head + d) % N_HEAD},
            device_id_type=MESH,
        )

    carry_copy = pltpu.make_async_remote_copy(
        src_ref=carry_buf.at[0],
        dst_ref=carry_buf.at[1],
        send_sem=c_send.at[0],
        recv_sem=c_recv.at[0],
        device_id={"seq": below},
        device_id_type=MESH,
    )
    far_first = sorted(range(1, RING), key=lambda d: -min(d, RING - d))

    lane = lax.broadcasted_iota(jnp.int32, (LOCAL_HEADS, TOKENS), 1)
    diagonal = lax.broadcasted_iota(jnp.int32, (LOCAL_HEADS, LOCAL_HEADS), 0) == lax.broadcasted_iota(
        jnp.int32, (LOCAL_HEADS, LOCAL_HEADS), 1
    )
    rate = jnp.sum(
        jnp.where(diagonal, jnp.broadcast_to(decay_ref[...], (LOCAL_HEADS, LOCAL_HEADS)), 0.0), axis=1, keepdims=True
    )
    cum = step_ref[...] * rate
    reach = 1
    while reach < TOKENS:
        cum = cum + jnp.where(lane >= reach, pltpu.roll(cum, reach, 1), 0.0)
        reach *= 2
    cum = cum * LOG2E
    cum_buf[...] = cum
    seg_row = seg_ref[...].astype(F32)
    seg_last = seg_row[:, TOKENS - 1 :]
    seg_first = seg_row[:, :1]
    last_cum = cum[:, TOKENS - 1 :]
    tail = jnp.where(seg_row == seg_last, jnp.exp2(jnp.minimum(cum - last_cum, 0.0)), 0.0)
    enter = jnp.where(seg_row == seg_first, jnp.exp2(-cum), 0.0)
    col_buf[...] = jnp.concatenate(
        [cum, tail, enter, jnp.zeros((128 - 3 * LOCAL_HEADS, TOKENS), F32)], axis=0
    ).T
    in_map = in_ref[...]
    in_map_t = in_map.astype(F32).T.astype(BF16)
    first_half = lax.broadcasted_iota(jnp.int32, (TOKENS, 128), 1) < HEAD_P

    def pair_columns(base, p):
        a = jnp.broadcast_to(col_buf[:, base + 2 * p : base + 2 * p + 1], (TOKENS, 128))
        b = jnp.broadcast_to(col_buf[:, base + 2 * p + 1 : base + 2 * p + 2], (TOKENS, 128))
        return jnp.where(first_half, a, b)

    block_decay = jnp.broadcast_to(jnp.exp2(-last_cum), (LOCAL_HEADS, 128))
    decay_hi = block_decay.astype(BF16).astype(F32)
    decay_lo = block_decay - decay_hi
    note_row = lax.broadcasted_iota(jnp.int32, (16, 128), 0)
    tags = jnp.where(
        note_row == 2,
        jnp.broadcast_to(seg_first, (16, 128)),
        jnp.where(note_row == 3, jnp.broadcast_to(seg_last, (16, 128)), 0.0),
    )
    for p in range(PAIRS):
        weighted = (x_ref[:, p * 128 : (p + 1) * 128].astype(F32) * pair_columns(LOCAL_HEADS, p)).astype(BF16)
        end_state = dot(in_map_t, weighted).T.astype(BF16)
        for half in range(2):
            h = 2 * p + half
            send_buf[h, :HEAD_P] = end_state[half * HEAD_P : (half + 1) * HEAD_P]
            note = jnp.where(
                note_row == 0,
                jnp.broadcast_to(decay_hi[h : h + 1], (16, 128)),
                jnp.where(note_row == 1, jnp.broadcast_to(decay_lo[h : h + 1], (16, 128)), tags),
            )
            send_buf[h, HEAD_P:] = note.astype(BF16)

    kt_buf[0, :HEAD_D] = k_ref[...].astype(F32).T.astype(BF16)
    documents = lax.broadcasted_iota(jnp.int32, (16, TOKENS), 0).astype(F32)
    kt_buf[0, HEAD_D:KT_ROWS] = jnp.where(documents == seg_row, 0.0, -FAR).astype(BF16)
    v_buf[0] = v_ref[...]
    for hop in range(DOC_SPAN + 1):
        kt_buf[hop, KT_ROWS:] = jnp.zeros((TOKENS - KT_ROWS, TOKENS), BF16)

    pl.semaphore_wait(barrier, RING - 1 + 4 + N_HEAD - 1)
    for d in far_first:
        scan_copy(d).start()
    for copy in kv_copies(0):
        copy.start()
    scan_buf[z] = send_buf[z]

    def forward(hop):
        for copy, onward in zip(kv_copies(hop - 1), kv_copies(hop) if hop < DOC_SPAN else (None, None)):
            copy.wait_recv()
            if onward is not None:
                onward.start()

    seg_col = jnp.broadcast_to(seg_row, (128, TOKENS)).T
    onehot_buf[...] = jnp.where(
        lax.broadcasted_iota(jnp.int32, (TOKENS, 128), 1).astype(F32) == seg_col, 1.0, 0.0
    ).astype(BF16)
    causal = lax.broadcasted_iota(jnp.int32, (TOKENS, TOKENS), 1) <= lax.broadcasted_iota(
        jnp.int32, (TOKENS, TOKENS), 0
    )
    same = jnp.concatenate([seg_col, seg_col], axis=1) == jnp.broadcast_to(seg_row, (TOKENS, TOKENS))
    g_buf[...] = jnp.where(causal & same, dot(out_ref[...], in_map, ((1,), (1,))), 0.0)

    def within(pairs):
        for p in pairs:
            x_pair = x_ref[:, p * 128 : (p + 1) * 128]
            zero = jnp.zeros_like(x_pair)
            total = jnp.zeros((TOKENS, 128), F32)
            for half in range(2):
                h = 2 * p + half
                gap = jnp.broadcast_to(cum_buf[h : h + 1, :], (TOKENS, TOKENS)) - jnp.broadcast_to(
                    col_buf[:, h : h + 1], (TOKENS, TOKENS)
                )
                mixing = (jnp.exp2(jnp.minimum(gap, 0.0)) * g_buf[...]).astype(BF16)
                x_half = jnp.where(first_half, x_pair, zero) if half == 0 else jnp.where(first_half, zero, x_pair)
                total = total + dot(mixing, x_half)
            skip = jnp.where(
                first_half[:1], skip_ref[:, 2 * p : 2 * p + 1], skip_ref[:, 2 * p + 1 : 2 * p + 2]
            )
            y_buf[p] = total + skip * x_pair.astype(F32)

    def attend(hops):
        first, final = hops[0] == 0, hops[-1] == DOC_SPAN

        def one(h, _):
            columns = pl.ds(pl.multiple_of(h * HEAD_D, HEAD_D), HEAD_D)
            q = jnp.concatenate([q_ref[:, columns], onehot_buf[...]], axis=1)
            scores = []
            for hop in hops:
                s = dot(q, kt_buf[hop])
                if hop == 0:
                    s = jnp.where(causal, s, -2.0 * FAR)
                scores.append(s)
            top = scores[0]
            for s in scores[1:]:
                top = jnp.maximum(top, s)
            best = jnp.broadcast_to(jnp.max(top, axis=1, keepdims=True), (TOKENS, 128))
            if not first:
                before = max_buf[h]
                best = jnp.maximum(before, best)
            best2 = jnp.concatenate([best, best], axis=1)
            ones = jnp.ones((TOKENS, HEAD_D), BF16)
            total = None
            for hop, s in zip(hops, scores):
                weights = jnp.exp2((s - best2) * SCORE_SCALE).astype(BF16)
                part = dot(weights, jnp.concatenate([v_buf[hop], ones], axis=1))
                total = part if total is None else total + part
            if not first:
                shrink = jnp.exp2((before - best) * SCORE_SCALE)
                total = total + acc_buf[h] * jnp.concatenate([shrink, shrink], axis=1)
            if final:
                att_ref[:, columns] = (total[:, :HEAD_D] / total[:, HEAD_D:]).astype(BF16)
            else:
                acc_buf[h] = total
                max_buf[h] = best
            return 0

        lax.fori_loop(0, LOCAL_ATT, one, 0)

    within(range(0, 4))
    forward(1)
    within(range(4, 8))
    forward(2)
    attend((0,))
    forward(3)
    attend((1, 2))

    for d in far_first:
        scan_copy(d).wait_recv()
    state = jnp.zeros((HEAD_P, STATE_N), F32)
    product = jnp.ones((1, STATE_N), F32)
    notes = []
    last_before = None
    for i in range(RING):
        block = scan_buf[i].astype(F32)
        decay = block[HEAD_P : HEAD_P + 1] + block[HEAD_P + 1 : HEAD_P + 2]
        tag_first, tag_last = block[HEAD_P + 2 : HEAD_P + 3], block[HEAD_P + 3 : HEAD_P + 4]
        if i >= DOC_SPAN:
            back_buf[i] = jnp.where(tag_first == last_before, state, 0.0).astype(BF16)
        else:
            local_buf[i] = state
            notes.append((product, tag_first, last_before))
        kept = decay if i == 0 else jnp.where(tag_last == last_before, decay, 0.0)
        state = block[:HEAD_P] + kept * state
        product = product * decay
        last_before = tag_last
    carry_buf[0, :HEAD_P] = state.astype(BF16)
    carry_buf[0, HEAD_P:] = jnp.broadcast_to(last_before, (16, STATE_N)).astype(BF16)
    carry_copy.start()
    for d in far_first:

        @pl.when((z + d) % RING >= DOC_SPAN)
        def _(d=d):
            back_copy(d).start()

    forward(4)
    carry_copy.wait_recv()
    carried = carry_buf[1, :HEAD_P].astype(F32)
    carried_tag = carry_buf[1, HEAD_P:].astype(F32)[:1]
    for i, (product, tag_first, last_before) in enumerate(notes):
        if i == 0:
            full = jnp.where(tag_first == carried_tag, carried, 0.0)
        else:
            full = local_buf[i] + jnp.where(carried_tag == last_before, product, 0.0) * carried
            full = jnp.where(tag_first == last_before, full, 0.0)
        back_buf[i] = full.astype(BF16)
    for d in far_first:

        @pl.when((z + d) % RING < DOC_SPAN)
        def _(d=d):
            back_copy(d).start()

    in_buf[z] = back_buf[z]
    forward(5)
    attend((3, 4))
    forward(6)
    attend((5, 6))
    forward(7)

    for d in far_first:
        back_copy(d).wait_recv()
    squares = jnp.zeros((TOKENS, 128), F32)
    for p in range(PAIRS):
        entering = jnp.concatenate([in_buf[2 * p], in_buf[2 * p + 1]], axis=0)
        incoming = dot(out_ref[...], entering, ((1,), (1,)))
        mixed = y_buf[p] + pair_columns(2 * LOCAL_HEADS, p) * incoming
        gate = gate_ref[:, p * 128 : (p + 1) * 128].astype(F32)
        gated = mixed * (gate / (1.0 + jnp.exp(-gate)))
        y_buf[p] = gated
        squares = squares + gated * gated
    squares_t = squares.T
    partial = squares_t[:8]
    for i in range(1, 16):
        partial = partial + squares_t[8 * i : 8 * i + 8]
    sq_buf[head] = partial
    for d in range(1, N_HEAD):
        square_copy(d).start()
    forward(8)
    attend((7, 8))
    for d in range(1, N_HEAD):
        square_copy(d).wait_recv()
    total = sq_buf[0]
    for i in range(1, N_HEAD):
        total = total + sq_buf[i]
    mean = jnp.sum(total, axis=0, keepdims=True) * (1.0 / (SSD_HEADS * HEAD_P))
    scale = jnp.broadcast_to(lax.rsqrt(mean + 1e-05), (128, TOKENS)).T
    for p in range(PAIRS):
        state_ref[:, p * 128 : (p + 1) * 128] = (
            y_buf[p] * scale * gain_ref[:, p * 128 : (p + 1) * 128]
        ).astype(BF16)

    for hop in range(DOC_SPAN):
        for copy in kv_copies(hop):
            copy.wait_send()
    for d in far_first:
        scan_copy(d).wait_send()
        back_copy(d).wait_send()
    for d in range(1, N_HEAD):
        square_copy(d).wait_send()
    carry_copy.wait_send()


def per_device(mixer_input, gate_input, input_map, output_map, step_size, decay_rate, skip_gain, norm_gain, queries, key_rows, values, segment):
    width = mixer_input.shape[1]
    vmem = pl.BlockSpec(memory_space=pltpu.VMEM)
    dma = pltpu.SemaphoreType.DMA
    out = jax.ShapeDtypeStruct((TOKENS, width), BF16)
    return pl.pallas_call(
        kernel,
        out_shape=(out, out),
        in_specs=[vmem] * 12,
        out_specs=(vmem, vmem),
        scratch_shapes=[
            pltpu.VMEM((DOC_SPAN + 1, TOKENS, TOKENS), BF16),
            pltpu.VMEM((DOC_SPAN + 1, TOKENS, HEAD_D), BF16),
            pltpu.VMEM((LOCAL_HEADS, MSG, STATE_N), BF16),
            pltpu.VMEM((RING, MSG, STATE_N), BF16),
            pltpu.VMEM((DOC_SPAN, HEAD_P, STATE_N), F32),
            pltpu.VMEM((RING, HEAD_P, STATE_N), BF16),
            pltpu.VMEM((2, MSG, STATE_N), BF16),
            pltpu.VMEM((LOCAL_HEADS, HEAD_P, STATE_N), BF16),
            pltpu.VMEM((N_HEAD, 8, TOKENS), F32),
            pltpu.VMEM((PAIRS, TOKENS, 128), F32),
            pltpu.VMEM((LOCAL_ATT, TOKENS, 2 * HEAD_D), F32),
            pltpu.VMEM((LOCAL_ATT, TOKENS, 128), F32),
            pltpu.VMEM((TOKENS, TOKENS), F32),
            pltpu.VMEM((TOKENS, 128), BF16),
            pltpu.VMEM((TOKENS, 128), F32),
            pltpu.VMEM((LOCAL_HEADS, TOKENS), F32),
            dma((DOC_SPAN,)),
            dma((DOC_SPAN,)),
            dma((DOC_SPAN,)),
            dma((DOC_SPAN,)),
            dma((RING,)),
            dma((RING,)),
            dma((1,)),
            dma((1,)),
            dma((RING,)),
            dma((RING,)),
            dma((N_HEAD,)),
            dma((N_HEAD,)),
        ],
        compiler_params=pltpu.CompilerParams(collective_id=0, has_side_effects=True, vmem_limit_bytes=40 * 2**20),
        cost_estimate=pl.CostEstimate(flops=3 * 10**9, bytes_accessed=4 * 10**6, transcendentals=6 * 10**6),
    )(
        mixer_input,
        gate_input,
        input_map,
        output_map,
        step_size,
        decay_rate[None, :],
        skip_gain[None, :],
        norm_gain[None, :],
        queries,
        key_rows,
        values,
        segment[None, :],
    )


def solution(mesh):
    in_specs = (
        P("seq", "head"),
        P("seq", "head"),
        P("seq", "head"),
        P("seq", "head"),
        P("head", "seq"),
        P("head"),
        P("head"),
        P("head"),
        P("seq", "head"),
        P("seq", "head"),
        P("seq", "head"),
        P("seq"),
    )
    out_specs = (P("seq", "head"), P("seq", "head"))
    return jax.shard_map(per_device, mesh=mesh, in_specs=in_specs, out_specs=out_specs, check_vma=False)
```

```python
import math

import jax
import jax.numpy as jnp
from jax import lax
from jax.experimental import pallas as pl
from jax.experimental.pallas import tpu as pltpu
from jax.sharding import PartitionSpec as P

SSD_HEADS = 128
HEAD_P = 64
STATE_N = 128
ATT_HEADS = 64
HEAD_D = 128
DOC_SPAN = 8
TOKENS = 256
N_SEQ = 64
RING = 16
N_HEAD = 8
LOCAL_HEADS = SSD_HEADS // N_HEAD
LOCAL_ATT = ATT_HEADS // N_HEAD
PAIRS = LOCAL_HEADS // 2
KT_ROWS = HEAD_D + 16
MSG = HEAD_P + 16
LOG2E = 1.0 / math.log(2.0)
SCORE_SCALE = LOG2E / math.sqrt(HEAD_D)
FAR = float(2**19)
MESH = pl.DeviceIdType.MESH
F32 = jnp.float32
BF16 = jnp.bfloat16


def dot(a, b, contract=((1,), (0,))):
    return lax.dot_general(a, b, (contract, ((), ())), preferred_element_type=F32)


def kernel(
    x_hbm, gate_hbm, in_hbm, out_hbm, step_hbm, decay_hbm, skip_hbm, gain_hbm, q_hbm, k_hbm, v_hbm, seg_hbm,
    state_ref, att_ref,
    x_ref, gate_ref, in_ref, out_ref, step_ref, decay_ref, skip_ref, gain_ref, q_ref, k_ref, v_ref, seg_ref, load_sem,
    kt_buf, v_buf, send_buf, scan_buf, local_buf, back_buf, carry_buf, in_buf, sq_buf,
    y_buf, enter_buf, acc_buf, max_buf, g_buf, onehot_buf, col_buf, cum_buf,
    kt_send, kt_recv, v_send, v_recv, a_send, a_recv, c_send, c_recv, b_send, b_recv, s_send, s_recv,
):
    me = lax.axis_index("seq")
    head = lax.axis_index("head")
    row, z = me // RING, me % RING
    succ, pred = (me + 1) % N_SEQ, (me + N_SEQ - 1) % N_SEQ
    below, above = (me + RING) % N_SEQ, (me + N_SEQ - RING) % N_SEQ

    def ring(d):
        return row * RING + (z + d) % RING

    barrier = pltpu.get_barrier_semaphore()
    for d in sorted(range(1, RING), key=lambda d: -min(d, RING - d)):
        pl.semaphore_signal(barrier, inc=1, device_id={"seq": ring(d)}, device_id_type=MESH)
    for other in (below, above, succ, pred):
        pl.semaphore_signal(barrier, inc=1, device_id={"seq": other}, device_id_type=MESH)
    for d in range(1, N_HEAD):
        pl.semaphore_signal(barrier, inc=1, device_id={"head": (head + d) % N_HEAD}, device_id_type=MESH)

    loads = {}
    for i, (name, source, target) in enumerate(
        (
            ("step", step_hbm, step_ref),
            ("decay", decay_hbm, decay_ref),
            ("seg", seg_hbm, seg_ref),
            ("in", in_hbm, in_ref),
            ("x", x_hbm, x_ref),
            ("k", k_hbm, k_ref),
            ("v", v_hbm, v_ref),
            ("out", out_hbm, out_ref),
            ("skip", skip_hbm, skip_ref),
            ("q", q_hbm, q_ref),
            ("gate", gate_hbm, gate_ref),
            ("gain", gain_hbm, gain_ref),
        )
    ):
        loads[name] = pltpu.make_async_copy(source, target, load_sem.at[i])
        loads[name].start()

    def loaded(*names):
        for name in names:
            loads[name].wait()

    def kv_copies(hop):
        return (
            pltpu.make_async_remote_copy(
                src_ref=kt_buf.at[hop, pl.ds(0, KT_ROWS)],
                dst_ref=kt_buf.at[hop + 1, pl.ds(0, KT_ROWS)],
                send_sem=kt_send.at[hop],
                recv_sem=kt_recv.at[hop],
                device_id={"seq": succ},
                device_id_type=MESH,
            ),
            pltpu.make_async_remote_copy(
                src_ref=v_buf.at[hop],
                dst_ref=v_buf.at[hop + 1],
                send_sem=v_send.at[hop],
                recv_sem=v_recv.at[hop],
                device_id={"seq": succ},
                device_id_type=MESH,
            ),
        )

    def scan_copy(d):
        return pltpu.make_async_remote_copy(
            src_ref=send_buf.at[(z + d) % RING],
            dst_ref=scan_buf.at[z],
            send_sem=a_send.at[d],
            recv_sem=a_recv.at[d],
            device_id={"seq": ring(d)},
            device_id_type=MESH,
        )

    def back_copy(d):
        return pltpu.make_async_remote_copy(
            src_ref=back_buf.at[(z + d) % RING],
            dst_ref=in_buf.at[z],
            send_sem=b_send.at[d],
            recv_sem=b_recv.at[d],
            device_id={"seq": ring(d)},
            device_id_type=MESH,
        )

    def square_copy(d):
        return pltpu.make_async_remote_copy(
            src_ref=sq_buf.at[head],
            dst_ref=sq_buf.at[head],
            send_sem=s_send.at[d],
            recv_sem=s_recv.at[d],
            device_id={"head": (head + d) % N_HEAD},
            device_id_type=MESH,
        )

    carry_copy = pltpu.make_async_remote_copy(
        src_ref=carry_buf.at[0],
        dst_ref=carry_buf.at[1],
        send_sem=c_send.at[0],
        recv_sem=c_recv.at[0],
        device_id={"seq": below},
        device_id_type=MESH,
    )
    far_first = sorted(range(1, RING), key=lambda d: -min(d, RING - d))

    loaded("step", "decay", "seg")
    lane = lax.broadcasted_iota(jnp.int32, (LOCAL_HEADS, TOKENS), 1)
    diagonal = lax.broadcasted_iota(jnp.int32, (LOCAL_HEADS, LOCAL_HEADS), 0) == lax.broadcasted_iota(
        jnp.int32, (LOCAL_HEADS, LOCAL_HEADS), 1
    )
    rate = jnp.sum(
        jnp.where(diagonal, jnp.broadcast_to(decay_ref[...], (LOCAL_HEADS, LOCAL_HEADS)), 0.0), axis=1, keepdims=True
    )
    cum = step_ref[...] * rate
    reach = 1
    while reach < TOKENS:
        cum = cum + jnp.where(lane >= reach, pltpu.roll(cum, reach, 1), 0.0)
        reach *= 2
    cum = cum * LOG2E
    cum_buf[...] = cum
    seg_row = seg_ref[...].astype(F32)
    seg_last = seg_row[:, TOKENS - 1 :]
    seg_first = seg_row[:, :1]
    last_cum = cum[:, TOKENS - 1 :]
    tail = jnp.where(seg_row == seg_last, jnp.exp2(jnp.minimum(cum - last_cum, 0.0)), 0.0)
    enter = jnp.where(seg_row == seg_first, jnp.exp2(-cum), 0.0)
    col_buf[...] = jnp.concatenate(
        [cum, tail, enter, jnp.zeros((128 - 3 * LOCAL_HEADS, TOKENS), F32)], axis=0
    ).T
    loaded("in", "x")
    in_map = in_ref[...]
    in_map_t = in_map.astype(F32).T.astype(BF16)
    first_half = lax.broadcasted_iota(jnp.int32, (TOKENS, 128), 1) < HEAD_P

    def pair_columns(base, p):
        a = jnp.broadcast_to(col_buf[:, base + 2 * p : base + 2 * p + 1], (TOKENS, 128))
        b = jnp.broadcast_to(col_buf[:, base + 2 * p + 1 : base + 2 * p + 2], (TOKENS, 128))
        return jnp.where(first_half, a, b)

    block_decay = jnp.broadcast_to(jnp.exp2(-last_cum), (LOCAL_HEADS, 128))
    decay_hi = block_decay.astype(BF16).astype(F32)
    decay_lo = block_decay - decay_hi
    note_row = lax.broadcasted_iota(jnp.int32, (16, 128), 0)
    tags = jnp.where(
        note_row == 2,
        jnp.broadcast_to(seg_first, (16, 128)),
        jnp.where(note_row == 3, jnp.broadcast_to(seg_last, (16, 128)), 0.0),
    )
    for p in range(PAIRS):
        weighted = (x_ref[:, p * 128 : (p + 1) * 128].astype(F32) * pair_columns(LOCAL_HEADS, p)).astype(BF16)
        end_state = dot(in_map_t, weighted).T.astype(BF16)
        for half in range(2):
            h = 2 * p + half
            send_buf[h, :HEAD_P] = end_state[half * HEAD_P : (half + 1) * HEAD_P]
            note = jnp.where(
                note_row == 0,
                jnp.broadcast_to(decay_hi[h : h + 1], (16, 128)),
                jnp.where(note_row == 1, jnp.broadcast_to(decay_lo[h : h + 1], (16, 128)), tags),
            )
            send_buf[h, HEAD_P:] = note.astype(BF16)

    loaded("k", "v")
    kt_buf[0, :HEAD_D] = k_ref[...].astype(F32).T.astype(BF16)
    documents = lax.broadcasted_iota(jnp.int32, (16, TOKENS), 0).astype(F32)
    kt_buf[0, HEAD_D:KT_ROWS] = jnp.where(documents == seg_row, 0.0, -FAR).astype(BF16)
    v_buf[0] = v_ref[...]
    for hop in range(DOC_SPAN + 1):
        kt_buf[hop, KT_ROWS:] = jnp.zeros((TOKENS - KT_ROWS, TOKENS), BF16)

    pl.semaphore_wait(barrier, RING - 1 + 4 + N_HEAD - 1)
    for d in far_first:
        scan_copy(d).start()
    for copy in kv_copies(0):
        copy.start()
    scan_buf[z] = send_buf[z]

    def forward(hop):
        for copy, onward in zip(kv_copies(hop - 1), kv_copies(hop) if hop < DOC_SPAN else (None, None)):
            copy.wait_recv()
            if onward is not None:
                onward.start()

    loaded("out", "skip", "q", "gate", "gain")
    seg_col = jnp.broadcast_to(seg_row, (128, TOKENS)).T
    onehot_buf[...] = jnp.where(
        lax.broadcasted_iota(jnp.int32, (TOKENS, 128), 1).astype(F32) == seg_col, 1.0, 0.0
    ).astype(BF16)
    causal = lax.broadcasted_iota(jnp.int32, (TOKENS, TOKENS), 1) <= lax.broadcasted_iota(
        jnp.int32, (TOKENS, TOKENS), 0
    )
    same = jnp.concatenate([seg_col, seg_col], axis=1) == jnp.broadcast_to(seg_row, (TOKENS, TOKENS))
    g_buf[...] = jnp.where(causal & same, dot(out_ref[...], in_map, ((1,), (1,))), 0.0)

    def within(pairs):
        for p in pairs:
            x_pair = x_ref[:, p * 128 : (p + 1) * 128]
            zero = jnp.zeros_like(x_pair)
            total = jnp.zeros((TOKENS, 128), F32)
            for half in range(2):
                h = 2 * p + half
                gap = jnp.broadcast_to(cum_buf[h : h + 1, :], (TOKENS, TOKENS)) - jnp.broadcast_to(
                    col_buf[:, h : h + 1], (TOKENS, TOKENS)
                )
                mixing = (jnp.exp2(jnp.minimum(gap, 0.0)) * g_buf[...]).astype(BF16)
                x_half = jnp.where(first_half, x_pair, zero) if half == 0 else jnp.where(first_half, zero, x_pair)
                total = total + dot(mixing, x_half)
            skip = jnp.where(
                first_half[:1], skip_ref[:, 2 * p : 2 * p + 1], skip_ref[:, 2 * p + 1 : 2 * p + 2]
            )
            gate = gate_ref[:, p * 128 : (p + 1) * 128].astype(F32)
            opened = gate / (1.0 + jnp.exp(-gate))
            y_buf[p] = (total + skip * x_pair.astype(F32)) * opened
            enter_buf[p] = pair_columns(2 * LOCAL_HEADS, p) * opened

    def attend(hops):
        first, final = hops[0] == 0, hops[-1] == DOC_SPAN

        def one(h, _):
            columns = pl.ds(pl.multiple_of(h * HEAD_D, HEAD_D), HEAD_D)
            q = jnp.concatenate([q_ref[:, columns], onehot_buf[...]], axis=1)
            scores = []
            for hop in hops:
                s = dot(q, kt_buf[hop])
                if hop == 0:
                    s = jnp.where(causal, s, -2.0 * FAR)
                scores.append(s)
            top = scores[0]
            for s in scores[1:]:
                top = jnp.maximum(top, s)
            best = jnp.broadcast_to(jnp.max(top, axis=1, keepdims=True), (TOKENS, 128))
            if not first:
                before = max_buf[h]
                best = jnp.maximum(before, best)
            best2 = jnp.concatenate([best, best], axis=1)
            ones = jnp.ones((TOKENS, HEAD_D), BF16)
            total = None
            for hop, s in zip(hops, scores):
                weights = jnp.exp2((s - best2) * SCORE_SCALE).astype(BF16)
                part = dot(weights, jnp.concatenate([v_buf[hop], ones], axis=1))
                total = part if total is None else total + part
            if not first:
                shrink = jnp.exp2((before - best) * SCORE_SCALE)
                total = total + acc_buf[h] * jnp.concatenate([shrink, shrink], axis=1)
            if final:
                att_ref[:, columns] = (total[:, :HEAD_D] / total[:, HEAD_D:]).astype(BF16)
            else:
                acc_buf[h] = total
                max_buf[h] = best
            return 0

        lax.fori_loop(0, LOCAL_ATT, one, 0, unroll=4)

    notes = []

    def scan():
        for d in far_first:
            scan_copy(d).wait_recv()
        state = jnp.zeros((HEAD_P, STATE_N), F32)
        product = jnp.ones((1, STATE_N), F32)
        last_before = None
        for i in range(RING):
            block = scan_buf[i].astype(F32)
            decay = block[HEAD_P : HEAD_P + 1] + block[HEAD_P + 1 : HEAD_P + 2]
            tag_first, tag_last = block[HEAD_P + 2 : HEAD_P + 3], block[HEAD_P + 3 : HEAD_P + 4]
            if i >= DOC_SPAN:
                back_buf[i] = jnp.where(tag_first == last_before, state, 0.0).astype(BF16)
            else:
                local_buf[i] = state
                notes.append((product, tag_first, last_before))
            kept = decay if i == 0 else jnp.where(tag_last == last_before, decay, 0.0)
            state = block[:HEAD_P] + kept * state
            product = product * decay
            last_before = tag_last
        carry_buf[0, :HEAD_P] = state.astype(BF16)
        carry_buf[0, HEAD_P:] = jnp.broadcast_to(last_before, (16, STATE_N)).astype(BF16)
        carry_copy.start()
        for d in far_first:

            @pl.when((z + d) % RING >= DOC_SPAN)
            def _(d=d):
                back_copy(d).start()


    def carry():
        carry_copy.wait_recv()
        carried = carry_buf[1, :HEAD_P].astype(F32)
        carried_tag = carry_buf[1, HEAD_P:].astype(F32)[:1]
        for i, (product, tag_first, last_before) in enumerate(notes):
            if i == 0:
                full = jnp.where(tag_first == carried_tag, carried, 0.0)
            else:
                full = local_buf[i] + jnp.where(carried_tag == last_before, product, 0.0) * carried
                full = jnp.where(tag_first == last_before, full, 0.0)
            back_buf[i] = full.astype(BF16)
        for d in far_first:

            @pl.when((z + d) % RING < DOC_SPAN)
            def _(d=d):
                back_copy(d).start()

        in_buf[z] = back_buf[z]

    def enter_block():
        for d in far_first:
            back_copy(d).wait_recv()
        squares = jnp.zeros((TOKENS, 128), F32)
        for p in range(PAIRS):
            entering = jnp.concatenate([in_buf[2 * p], in_buf[2 * p + 1]], axis=0)
            incoming = dot(out_ref[...], entering, ((1,), (1,)))
            gated = y_buf[p] + enter_buf[p] * incoming
            y_buf[p] = gated
            squares = squares + gated * gated
        squares_t = squares.T
        partial = squares_t[:8]
        for i in range(1, 16):
            partial = partial + squares_t[8 * i : 8 * i + 8]
        sq_buf[head] = partial
        for d in range(1, N_HEAD):
            square_copy(d).start()

    def normalise():
        for d in range(1, N_HEAD):
            square_copy(d).wait_recv()
        total = sq_buf[0]
        for i in range(1, N_HEAD):
            total = total + sq_buf[i]
        mean = jnp.sum(total, axis=0, keepdims=True) * (1.0 / (SSD_HEADS * HEAD_P))
        scale = jnp.broadcast_to(lax.rsqrt(mean + 1e-05), (128, TOKENS)).T
        for p in range(PAIRS):
            state_ref[:, p * 128 : (p + 1) * 128] = (
                y_buf[p] * scale * gain_ref[:, p * 128 : (p + 1) * 128]
            ).astype(BF16)


    within(range(0, 4))
    forward(1)
    within(range(4, 8))
    forward(2)
    attend((0,))
    attend((1, 2,))
    scan()
    forward(3)
    carry()
    forward(4)
    attend((3, 4,))
    forward(5)
    forward(6)
    attend((5, 6,))
    enter_block()
    forward(7)
    forward(8)
    attend((7, 8,))
    normalise()

    for hop in range(DOC_SPAN):
        for copy in kv_copies(hop):
            copy.wait_send()
    for d in far_first:
        scan_copy(d).wait_send()
        back_copy(d).wait_send()
    for d in range(1, N_HEAD):
        square_copy(d).wait_send()
    carry_copy.wait_send()


def per_device(mixer_input, gate_input, input_map, output_map, step_size, decay_rate, skip_gain, norm_gain, queries, key_rows, values, segment):
    width = mixer_input.shape[1]
    vmem = pl.BlockSpec(memory_space=pltpu.VMEM)
    dma = pltpu.SemaphoreType.DMA
    out = jax.ShapeDtypeStruct((TOKENS, width), BF16)
    operands = (
        mixer_input,
        gate_input,
        input_map,
        output_map,
        step_size,
        decay_rate[None, :],
        skip_gain[None, :],
        norm_gain[None, :],
        queries,
        key_rows,
        values,
        segment[None, :],
    )
    return pl.pallas_call(
        kernel,
        out_shape=(out, out),
        in_specs=[pl.BlockSpec(memory_space=pl.ANY)] * 12,
        out_specs=(vmem, vmem),
        scratch_shapes=[
            *(pltpu.VMEM(a.shape, a.dtype) for a in operands),
            dma((len(operands),)),
            pltpu.VMEM((DOC_SPAN + 1, TOKENS, TOKENS), BF16),
            pltpu.VMEM((DOC_SPAN + 1, TOKENS, HEAD_D), BF16),
            pltpu.VMEM((LOCAL_HEADS, MSG, STATE_N), BF16),
            pltpu.VMEM((RING, MSG, STATE_N), BF16),
            pltpu.VMEM((DOC_SPAN, HEAD_P, STATE_N), F32),
            pltpu.VMEM((RING, HEAD_P, STATE_N), BF16),
            pltpu.VMEM((2, MSG, STATE_N), BF16),
            pltpu.VMEM((LOCAL_HEADS, HEAD_P, STATE_N), BF16),
            pltpu.VMEM((N_HEAD, 8, TOKENS), F32),
            pltpu.VMEM((PAIRS, TOKENS, 128), F32),
            pltpu.VMEM((PAIRS, TOKENS, 128), F32),
            pltpu.VMEM((LOCAL_ATT, TOKENS, 2 * HEAD_D), F32),
            pltpu.VMEM((LOCAL_ATT, TOKENS, 128), F32),
            pltpu.VMEM((TOKENS, TOKENS), F32),
            pltpu.VMEM((TOKENS, 128), BF16),
            pltpu.VMEM((TOKENS, 128), F32),
            pltpu.VMEM((LOCAL_HEADS, TOKENS), F32),
            dma((DOC_SPAN,)),
            dma((DOC_SPAN,)),
            dma((DOC_SPAN,)),
            dma((DOC_SPAN,)),
            dma((RING,)),
            dma((RING,)),
            dma((1,)),
            dma((1,)),
            dma((RING,)),
            dma((RING,)),
            dma((N_HEAD,)),
            dma((N_HEAD,)),
        ],
        compiler_params=pltpu.CompilerParams(collective_id=0, has_side_effects=True, vmem_limit_bytes=56 * 2**20),
        cost_estimate=pl.CostEstimate(flops=3 * 10**9, bytes_accessed=4 * 10**6, transcendentals=6 * 10**6),
    )(*operands)


def solution(mesh):
    in_specs = (
        P("seq", "head"),
        P("seq", "head"),
        P("seq", "head"),
        P("seq", "head"),
        P("head", "seq"),
        P("head"),
        P("head"),
        P("head"),
        P("seq", "head"),
        P("seq", "head"),
        P("seq", "head"),
        P("seq"),
    )
    out_specs = (P("seq", "head"), P("seq", "head"))
    return jax.shard_map(per_device, mesh=mesh, in_specs=in_specs, out_specs=out_specs, check_vma=False)
```

```python
import math

import jax
import jax.numpy as jnp
from jax import lax
from jax.experimental import pallas as pl
from jax.experimental.pallas import tpu as pltpu
from jax.sharding import PartitionSpec as P

SSD_HEADS = 128
HEAD_P = 64
STATE_N = 128
ATT_HEADS = 64
HEAD_D = 128
DOC_SPAN = 8
TOKENS = 256
N_SEQ = 64
RING = 16
RELAYED = (7, 8)
N_HEAD = 8
LOCAL_HEADS = SSD_HEADS // N_HEAD
LOCAL_ATT = ATT_HEADS // N_HEAD
PAIRS = LOCAL_HEADS // 2
KT_ROWS = HEAD_D + 16
MSG = HEAD_P + 16
LOG2E = 1.0 / math.log(2.0)
SCORE_SCALE = LOG2E / math.sqrt(HEAD_D)
FAR = float(2**19)
MESH = pl.DeviceIdType.MESH
F32 = jnp.float32
BF16 = jnp.bfloat16


def dot(a, b, contract=((1,), (0,))):
    return lax.dot_general(a, b, (contract, ((), ())), preferred_element_type=F32)


def kernel(
    x_hbm, gate_hbm, in_hbm, out_hbm, step_hbm, decay_hbm, skip_hbm, gain_hbm, q_hbm, k_hbm, v_hbm, seg_hbm,
    state_ref, att_ref,
    x_ref, gate_ref, in_ref, out_ref, step_ref, decay_ref, skip_ref, gain_ref, q_ref, k_ref, v_ref, seg_ref, load_sem,
    kt_buf, v_buf, send_buf, scan_buf, note_buf, relay_buf, local_buf, back_buf, carry_buf, in_buf, sq_buf,
    y_buf, enter_buf, acc_buf, max_buf, g_buf, onehot_buf, col_buf, cum_buf,
    kv_send, kv_recv, n_send, n_recv, r_send, r_recv, f_send, a_send, a_recv, c_send, c_recv, b_send, b_recv, s_send, s_recv,
):
    me = lax.axis_index("seq")
    head = lax.axis_index("head")
    row, z = me // RING, me % RING
    succ, pred = (me + 1) % N_SEQ, (me + N_SEQ - 1) % N_SEQ
    below, above = (me + RING) % N_SEQ, (me + N_SEQ - RING) % N_SEQ

    def ring(d):
        return row * RING + (z + d) % RING

    barrier = pltpu.get_barrier_semaphore()
    for d in sorted(range(1, RING), key=lambda d: -min(d, RING - d)):
        pl.semaphore_signal(barrier, inc=1, device_id={"seq": ring(d)}, device_id_type=MESH)
    for other in (below, above, succ, pred):
        pl.semaphore_signal(barrier, inc=1, device_id={"seq": other}, device_id_type=MESH)
    for d in range(1, N_HEAD):
        pl.semaphore_signal(barrier, inc=1, device_id={"head": (head + d) % N_HEAD}, device_id_type=MESH)

    loads = {}
    for i, (name, source, target) in enumerate(
        (
            ("step", step_hbm, step_ref),
            ("decay", decay_hbm, decay_ref),
            ("seg", seg_hbm, seg_ref),
            ("in", in_hbm, in_ref),
            ("x", x_hbm, x_ref),
            ("k", k_hbm, k_ref),
            ("v", v_hbm, v_ref),
            ("out", out_hbm, out_ref),
            ("skip", skip_hbm, skip_ref),
            ("q", q_hbm, q_ref),
            ("gate", gate_hbm, gate_ref),
            ("gain", gain_hbm, gain_ref),
        )
    ):
        loads[name] = pltpu.make_async_copy(source, target, load_sem.at[i])
        loads[name].start()

    def loaded(*names):
        for name in names:
            loads[name].wait()

    def kv_copies(hop):
        return [
            pltpu.make_async_remote_copy(
                src_ref=buf.at[hop, pl.ds(start, size)],
                dst_ref=buf.at[hop + 1, pl.ds(start, size)],
                send_sem=kv_send.at[hop, i],
                recv_sem=kv_recv.at[hop, i],
                device_id={"seq": succ},
                device_id_type=MESH,
            )
            for i, (buf, start, size) in enumerate(
                (
                    (kt_buf, 0, KT_ROWS - 64),
                    (kt_buf, KT_ROWS - 64, 64),
                    (v_buf, 0, TOKENS // 2),
                    (v_buf, TOKENS // 2, TOKENS // 2),
                )
            )
        ]

    def scan_copy(d):
        return pltpu.make_async_remote_copy(
            src_ref=send_buf.at[(z + d) % RING],
            dst_ref=scan_buf.at[z],
            send_sem=a_send.at[d],
            recv_sem=a_recv.at[d],
            device_id={"seq": ring(d)},
            device_id_type=MESH,
        )

    def back_copy(d):
        return pltpu.make_async_remote_copy(
            src_ref=back_buf.at[(z + d) % RING],
            dst_ref=in_buf.at[z],
            send_sem=b_send.at[d],
            recv_sem=b_recv.at[d],
            device_id={"seq": ring(d)},
            device_id_type=MESH,
        )

    def square_copy(d):
        return pltpu.make_async_remote_copy(
            src_ref=sq_buf.at[head],
            dst_ref=sq_buf.at[head],
            send_sem=s_send.at[d],
            recv_sem=s_recv.at[d],
            device_id={"head": (head + d) % N_HEAD},
            device_id_type=MESH,
        )

    def note_copy(d):
        return pltpu.make_async_remote_copy(
            src_ref=note_buf.at[z],
            dst_ref=note_buf.at[z],
            send_sem=n_send.at[d],
            recv_sem=n_recv.at[d],
            device_id={"seq": ring(d)},
            device_id_type=MESH,
        )

    def relay_out(phase, far):
        return pltpu.make_async_remote_copy(
            src_ref=(send_buf, back_buf)[phase].at[(z + far) % RING],
            dst_ref=relay_buf.at[phase, far - RELAYED[0]],
            send_sem=r_send.at[phase, far - RELAYED[0]],
            recv_sem=r_recv.at[phase, far - RELAYED[0]],
            device_id={"seq": ring(RING - RING // 4)},
            device_id_type=MESH,
        )

    def relay_on(phase, far):
        return pltpu.make_async_remote_copy(
            src_ref=relay_buf.at[phase, far - RELAYED[0]],
            dst_ref=(scan_buf, in_buf)[phase].at[(z + RING // 4) % RING],
            send_sem=f_send.at[phase, far - RELAYED[0]],
            recv_sem=(a_recv, b_recv)[phase].at[far],
            device_id={"seq": ring(far + RING // 4)},
            device_id_type=MESH,
        )

    def relay(phase):
        for far in RELAYED:
            relay_out(phase, far).wait_recv()
            relay_on(phase, far).start()

    carry_copy = pltpu.make_async_remote_copy(
        src_ref=carry_buf.at[0],
        dst_ref=carry_buf.at[1],
        send_sem=c_send.at[0],
        recv_sem=c_recv.at[0],
        device_id={"seq": below},
        device_id_type=MESH,
    )
    far_first = sorted((d for d in range(1, RING) if d not in RELAYED), key=lambda d: -min(d, RING - d))

    loaded("step", "decay", "seg")
    lane = lax.broadcasted_iota(jnp.int32, (LOCAL_HEADS, TOKENS), 1)
    diagonal = lax.broadcasted_iota(jnp.int32, (LOCAL_HEADS, LOCAL_HEADS), 0) == lax.broadcasted_iota(
        jnp.int32, (LOCAL_HEADS, LOCAL_HEADS), 1
    )
    rate = jnp.sum(
        jnp.where(diagonal, jnp.broadcast_to(decay_ref[...], (LOCAL_HEADS, LOCAL_HEADS)), 0.0), axis=1, keepdims=True
    )
    cum = step_ref[...] * rate
    reach = 1
    while reach < TOKENS:
        cum = cum + jnp.where(lane >= reach, pltpu.roll(cum, reach, 1), 0.0)
        reach *= 2
    cum = cum * LOG2E
    cum_buf[...] = cum
    seg_row = seg_ref[...].astype(F32)
    seg_last = seg_row[:, TOKENS - 1 :]
    seg_first = seg_row[:, :1]
    last_cum = cum[:, TOKENS - 1 :]
    tail = jnp.where(seg_row == seg_last, jnp.exp2(jnp.minimum(cum - last_cum, 0.0)), 0.0)
    enter = jnp.where(seg_row == seg_first, jnp.exp2(-cum), 0.0)
    col_buf[...] = jnp.concatenate(
        [cum, tail, enter, jnp.zeros((128 - 3 * LOCAL_HEADS, TOKENS), F32)], axis=0
    ).T
    loaded("in", "x")
    in_map = in_ref[...]
    in_map_t = in_map.astype(F32).T.astype(BF16)
    first_half = lax.broadcasted_iota(jnp.int32, (TOKENS, 128), 1) < HEAD_P

    def pair_columns(base, p):
        a = jnp.broadcast_to(col_buf[:, base + 2 * p : base + 2 * p + 1], (TOKENS, 128))
        b = jnp.broadcast_to(col_buf[:, base + 2 * p + 1 : base + 2 * p + 2], (TOKENS, 128))
        return jnp.where(first_half, a, b)

    note_lane = lax.broadcasted_iota(jnp.int32, (1, 128), 1)
    note_buf[z] = jnp.where(
        note_lane < LOCAL_HEADS,
        jnp.exp2(-col_buf[TOKENS - 1 :, :]),
        jnp.where(note_lane == LOCAL_HEADS, seg_first, seg_last),
    )
    for p in range(PAIRS):
        weighted = (x_ref[:, p * 128 : (p + 1) * 128].astype(F32) * pair_columns(LOCAL_HEADS, p)).astype(BF16)
        end_state = dot(in_map_t, weighted).T.astype(BF16)
        for half in range(2):
            h = 2 * p + half
            send_buf[h] = end_state[half * HEAD_P : (half + 1) * HEAD_P]

    loaded("k", "v")
    kt_buf[0, :HEAD_D] = k_ref[...].astype(F32).T.astype(BF16)
    documents = lax.broadcasted_iota(jnp.int32, (16, TOKENS), 0).astype(F32)
    kt_buf[0, HEAD_D:KT_ROWS] = jnp.where(documents == seg_row, 0.0, -FAR).astype(BF16)
    v_buf[0] = v_ref[...]
    for hop in range(DOC_SPAN + 1):
        kt_buf[hop, KT_ROWS:] = jnp.zeros((TOKENS - KT_ROWS, TOKENS), BF16)

    pl.semaphore_wait(barrier, RING - 1 + 4 + N_HEAD - 1)
    for far in RELAYED:
        relay_out(0, far).start()
    for d in far_first:
        scan_copy(d).start()
    for d in range(1, RING):
        note_copy(d).start()
    for copy in kv_copies(0):
        copy.start()
    scan_buf[z] = send_buf[z]

    def forward(hop):
        for copy, onward in zip(kv_copies(hop - 1), kv_copies(hop) if hop < DOC_SPAN else [None] * 4):
            copy.wait_recv()
            if onward is not None:
                onward.start()

    loaded("out", "skip", "q", "gate", "gain")
    seg_col = jnp.broadcast_to(seg_row, (128, TOKENS)).T
    onehot_buf[...] = jnp.where(
        lax.broadcasted_iota(jnp.int32, (TOKENS, 128), 1).astype(F32) == seg_col, 1.0, 0.0
    ).astype(BF16)
    causal = lax.broadcasted_iota(jnp.int32, (TOKENS, TOKENS), 1) <= lax.broadcasted_iota(
        jnp.int32, (TOKENS, TOKENS), 0
    )
    same = jnp.concatenate([seg_col, seg_col], axis=1) == jnp.broadcast_to(seg_row, (TOKENS, TOKENS))
    g_buf[...] = jnp.where(causal & same, dot(out_ref[...], in_map, ((1,), (1,))), 0.0)

    def within(pairs):
        for p in pairs:
            x_pair = x_ref[:, p * 128 : (p + 1) * 128]
            zero = jnp.zeros_like(x_pair)
            total = jnp.zeros((TOKENS, 128), F32)
            for half in range(2):
                h = 2 * p + half
                gap = jnp.broadcast_to(cum_buf[h : h + 1, :], (TOKENS, TOKENS)) - jnp.broadcast_to(
                    col_buf[:, h : h + 1], (TOKENS, TOKENS)
                )
                mixing = (jnp.exp2(jnp.minimum(gap, 0.0)) * g_buf[...]).astype(BF16)
                x_half = jnp.where(first_half, x_pair, zero) if half == 0 else jnp.where(first_half, zero, x_pair)
                total = total + dot(mixing, x_half)
            skip = jnp.where(
                first_half[:1], skip_ref[:, 2 * p : 2 * p + 1], skip_ref[:, 2 * p + 1 : 2 * p + 2]
            )
            gate = gate_ref[:, p * 128 : (p + 1) * 128].astype(F32)
            opened = gate / (1.0 + jnp.exp(-gate))
            y_buf[p] = (total + skip * x_pair.astype(F32)) * opened
            enter_buf[p] = pair_columns(2 * LOCAL_HEADS, p) * opened

    def attend(hops):
        first, final = hops[0] == 0, hops[-1] == DOC_SPAN

        def one(h, _):
            columns = pl.ds(pl.multiple_of(h * HEAD_D, HEAD_D), HEAD_D)
            q = jnp.concatenate([q_ref[:, columns], onehot_buf[...]], axis=1)
            scores = []
            for hop in hops:
                s = dot(q, kt_buf[hop])
                if hop == 0:
                    s = jnp.where(causal, s, -2.0 * FAR)
                scores.append(s)
            top = scores[0]
            for s in scores[1:]:
                top = jnp.maximum(top, s)
            best = jnp.broadcast_to(jnp.max(top, axis=1, keepdims=True), (TOKENS, 128))
            if not first:
                before = max_buf[h]
                best = jnp.maximum(before, best)
            best2 = jnp.concatenate([best, best], axis=1)
            ones = jnp.ones((TOKENS, HEAD_D), BF16)
            total = None
            for hop, s in zip(hops, scores):
                weights = jnp.exp2((s - best2) * SCORE_SCALE).astype(BF16)
                part = dot(weights, jnp.concatenate([v_buf[hop], ones], axis=1))
                total = part if total is None else total + part
            if not first:
                shrink = jnp.exp2((before - best) * SCORE_SCALE)
                total = total + acc_buf[h] * jnp.concatenate([shrink, shrink], axis=1)
            if final:
                att_ref[:, columns] = (total[:, :HEAD_D] / total[:, HEAD_D:]).astype(BF16)
            else:
                acc_buf[h] = total
                max_buf[h] = best
            return 0

        lax.fori_loop(0, LOCAL_ATT, one, 0, unroll=4)

    notes = []

    def scan():
        for d in far_first:
            scan_copy(d).wait_recv()
        for far in RELAYED:
            relay_on(0, far).wait_recv()
        for d in range(1, RING):
            note_copy(d).wait_recv()
        all_notes = jnp.concatenate([note_buf[i] for i in range(RING)], axis=0)
        decays = jnp.sum(
            jnp.where(lax.broadcasted_iota(jnp.int32, (RING, 128), 1) == z, all_notes, 0.0), axis=1, keepdims=True
        )
        decays = jnp.broadcast_to(decays, (RING, STATE_N))
        firsts = jnp.broadcast_to(all_notes[:, LOCAL_HEADS : LOCAL_HEADS + 1], (RING, STATE_N))
        lasts = jnp.broadcast_to(all_notes[:, LOCAL_HEADS + 1 : LOCAL_HEADS + 2], (RING, STATE_N))
        state = jnp.zeros((HEAD_P, STATE_N), F32)
        product = jnp.ones((1, STATE_N), F32)
        last_before = None
        for i in range(RING):
            block = scan_buf[i].astype(F32)
            decay, tag_first, tag_last = decays[i : i + 1], firsts[i : i + 1], lasts[i : i + 1]
            if i >= DOC_SPAN:
                back_buf[i] = jnp.where(tag_first == last_before, state, 0.0).astype(BF16)
            else:
                local_buf[i] = state
                notes.append((product, tag_first, last_before))
            kept = decay if i == 0 else jnp.where(tag_last == last_before, decay, 0.0)
            state = block + kept * state
            product = product * decay
            last_before = tag_last
        carry_buf[0, :HEAD_P] = state.astype(BF16)
        carry_buf[0, HEAD_P:] = jnp.broadcast_to(last_before, (16, STATE_N)).astype(BF16)
        carry_copy.start()

        for far in RELAYED:

            @pl.when((z + far) % RING >= DOC_SPAN)
            def _(far=far):
                relay_out(1, far).start()

        for d in far_first:

            @pl.when((z + d) % RING >= DOC_SPAN)
            def _(d=d):
                back_copy(d).start()


    def carry():
        carry_copy.wait_recv()
        carried = carry_buf[1, :HEAD_P].astype(F32)
        carried_tag = carry_buf[1, HEAD_P:].astype(F32)[:1]
        for i, (product, tag_first, last_before) in enumerate(notes):
            if i == 0:
                full = jnp.where(tag_first == carried_tag, carried, 0.0)
            else:
                full = local_buf[i] + jnp.where(carried_tag == last_before, product, 0.0) * carried
                full = jnp.where(tag_first == last_before, full, 0.0)
            back_buf[i] = full.astype(BF16)

        for far in RELAYED:

            @pl.when((z + far) % RING < DOC_SPAN)
            def _(far=far):
                relay_out(1, far).start()

        for d in far_first:

            @pl.when((z + d) % RING < DOC_SPAN)
            def _(d=d):
                back_copy(d).start()

        in_buf[z] = back_buf[z]

    def enter_block():
        for d in far_first:
            back_copy(d).wait_recv()
        for far in RELAYED:
            relay_on(1, far).wait_recv()
        squares = jnp.zeros((TOKENS, 128), F32)
        for p in range(PAIRS):
            entering = jnp.concatenate([in_buf[2 * p], in_buf[2 * p + 1]], axis=0)
            incoming = dot(out_ref[...], entering, ((1,), (1,)))
            gated = y_buf[p] + enter_buf[p] * incoming
            y_buf[p] = gated
            squares = squares + gated * gated
        squares_t = squares.T
        partial = squares_t[:8]
        for i in range(1, 16):
            partial = partial + squares_t[8 * i : 8 * i + 8]
        sq_buf[head] = partial
        for d in range(1, N_HEAD):
            square_copy(d).start()

    def normalise():
        for d in range(1, N_HEAD):
            square_copy(d).wait_recv()
        total = sq_buf[0]
        for i in range(1, N_HEAD):
            total = total + sq_buf[i]
        mean = jnp.sum(total, axis=0, keepdims=True) * (1.0 / (SSD_HEADS * HEAD_P))
        scale = jnp.broadcast_to(lax.rsqrt(mean + 1e-05), (128, TOKENS)).T
        for p in range(PAIRS):
            state_ref[:, p * 128 : (p + 1) * 128] = (
                y_buf[p] * scale * gain_ref[:, p * 128 : (p + 1) * 128]
            ).astype(BF16)


    forward(1)
    relay(0)
    within(range(0, 8))
    forward(2)
    attend((0,))
    attend((1,))
    scan()
    forward(3)
    attend((2,))
    carry()
    forward(4)
    relay(1)
    attend((3, 4))
    forward(5)
    attend((5,))
    forward(6)
    attend((6,))
    enter_block()
    forward(7)
    attend((7,))
    forward(8)
    attend((8,))
    normalise()

    for hop in range(DOC_SPAN):
        for copy in kv_copies(hop):
            copy.wait_send()
    for d in far_first:
        scan_copy(d).wait_send()
        back_copy(d).wait_send()
    for d in range(1, N_HEAD):
        square_copy(d).wait_send()
    carry_copy.wait_send()
    for phase in range(2):
        for far in RELAYED:
            relay_out(phase, far).wait_send()
            relay_on(phase, far).wait_send()
    for d in range(1, RING):
        note_copy(d).wait_send()


def per_device(mixer_input, gate_input, input_map, output_map, step_size, decay_rate, skip_gain, norm_gain, queries, key_rows, values, segment):
    width = mixer_input.shape[1]
    vmem = pl.BlockSpec(memory_space=pltpu.VMEM)
    dma = pltpu.SemaphoreType.DMA
    out = jax.ShapeDtypeStruct((TOKENS, width), BF16)
    operands = (
        mixer_input,
        gate_input,
        input_map,
        output_map,
        step_size,
        decay_rate[None, :],
        skip_gain[None, :],
        norm_gain[None, :],
        queries,
        key_rows,
        values,
        segment[None, :],
    )
    return pl.pallas_call(
        kernel,
        out_shape=(out, out),
        in_specs=[pl.BlockSpec(memory_space=pl.ANY)] * 12,
        out_specs=(vmem, vmem),
        scratch_shapes=[
            *(pltpu.VMEM(a.shape, a.dtype) for a in operands),
            dma((len(operands),)),
            pltpu.VMEM((DOC_SPAN + 1, TOKENS, TOKENS), BF16),
            pltpu.VMEM((DOC_SPAN + 1, TOKENS, HEAD_D), BF16),
            pltpu.VMEM((LOCAL_HEADS, HEAD_P, STATE_N), BF16),
            pltpu.VMEM((RING, HEAD_P, STATE_N), BF16),
            pltpu.VMEM((RING, 1, 128), F32),
            pltpu.VMEM((2, len(RELAYED), HEAD_P, STATE_N), BF16),
            pltpu.VMEM((DOC_SPAN, HEAD_P, STATE_N), F32),
            pltpu.VMEM((RING, HEAD_P, STATE_N), BF16),
            pltpu.VMEM((2, MSG, STATE_N), BF16),
            pltpu.VMEM((LOCAL_HEADS, HEAD_P, STATE_N), BF16),
            pltpu.VMEM((N_HEAD, 8, TOKENS), F32),
            pltpu.VMEM((PAIRS, TOKENS, 128), F32),
            pltpu.VMEM((PAIRS, TOKENS, 128), F32),
            pltpu.VMEM((LOCAL_ATT, TOKENS, 2 * HEAD_D), F32),
            pltpu.VMEM((LOCAL_ATT, TOKENS, 128), F32),
            pltpu.VMEM((TOKENS, TOKENS), F32),
            pltpu.VMEM((TOKENS, 128), BF16),
            pltpu.VMEM((TOKENS, 128), F32),
            pltpu.VMEM((LOCAL_HEADS, TOKENS), F32),
            dma((DOC_SPAN, 4)),
            dma((DOC_SPAN, 4)),
            dma((RING,)),
            dma((RING,)),
            dma((2, len(RELAYED))),
            dma((2, len(RELAYED))),
            dma((2, len(RELAYED))),
            dma((RING,)),
            dma((RING,)),
            dma((1,)),
            dma((1,)),
            dma((RING,)),
            dma((RING,)),
            dma((N_HEAD,)),
            dma((N_HEAD,)),
        ],
        compiler_params=pltpu.CompilerParams(collective_id=0, has_side_effects=True, vmem_limit_bytes=56 * 2**20),
        cost_estimate=pl.CostEstimate(flops=3 * 10**9, bytes_accessed=4 * 10**6, transcendentals=6 * 10**6),
    )(*operands)


def solution(mesh):
    in_specs = (
        P("seq", "head"),
        P("seq", "head"),
        P("seq", "head"),
        P("seq", "head"),
        P("head", "seq"),
        P("head"),
        P("head"),
        P("head"),
        P("seq", "head"),
        P("seq", "head"),
        P("seq", "head"),
        P("seq"),
    )
    out_specs = (P("seq", "head"), P("seq", "head"))
    return jax.shard_map(per_device, mesh=mesh, in_specs=in_specs, out_specs=out_specs, check_vma=False)
```

```python
import math

import jax
import jax.numpy as jnp
from jax import lax
from jax.experimental import pallas as pl
from jax.experimental.pallas import tpu as pltpu
from jax.sharding import PartitionSpec as P

SSD_HEADS = 128
HEAD_P = 64
STATE_N = 128
ATT_HEADS = 64
HEAD_D = 128
DOC_SPAN = 8
TOKENS = 256
N_SEQ = 64
RING = 16
RELAYED = ((7, 8), (7, 8))
N_HEAD = 8
LOCAL_HEADS = SSD_HEADS // N_HEAD
LOCAL_ATT = ATT_HEADS // N_HEAD
PAIRS = LOCAL_HEADS // 2
KT_ROWS = HEAD_D + 16
MSG = HEAD_P + 16
LOG2E = 1.0 / math.log(2.0)
SCORE_SCALE = LOG2E / math.sqrt(HEAD_D)
FAR = float(2**19)
MESH = pl.DeviceIdType.MESH
F32 = jnp.float32
BF16 = jnp.bfloat16


def dot(a, b, contract=((1,), (0,))):
    return lax.dot_general(a, b, (contract, ((), ())), preferred_element_type=F32)


def kernel(
    x_hbm, gate_hbm, in_hbm, out_hbm, step_hbm, decay_hbm, skip_hbm, gain_hbm, q_hbm, k_hbm, v_hbm, seg_hbm,
    state_ref, att_ref,
    x_ref, gate_ref, in_ref, out_ref, step_ref, decay_ref, skip_ref, gain_ref, q_ref, k_ref, v_ref, seg_ref, load_sem,
    kt_buf, v_buf, tag_buf, send_buf, scan_buf, note_buf, relay_buf, local_buf, back_buf, carry_buf, in_buf, sq_buf,
    y_buf, enter_buf, acc_buf, max_buf, g_buf, onehot_buf, col_buf, cum_buf,
    kv_send, kv_recv, n_send, n_recv, r_send, r_recv, f_send, a_send, a_recv, c_send, c_recv, b_send, b_recv, s_send, s_recv,
):
    me = lax.axis_index("seq")
    head = lax.axis_index("head")
    row, z = me // RING, me % RING
    succ, pred = (me + 1) % N_SEQ, (me + N_SEQ - 1) % N_SEQ
    below, above = (me + RING) % N_SEQ, (me + N_SEQ - RING) % N_SEQ

    def ring(d):
        return row * RING + (z + d) % RING

    barrier = pltpu.get_barrier_semaphore()
    for d in sorted(range(1, RING), key=lambda d: -min(d, RING - d)):
        pl.semaphore_signal(barrier, inc=1, device_id={"seq": ring(d)}, device_id_type=MESH)
    for other in (below, above, succ, pred):
        pl.semaphore_signal(barrier, inc=1, device_id={"seq": other}, device_id_type=MESH)
    for d in range(1, N_HEAD):
        pl.semaphore_signal(barrier, inc=1, device_id={"head": (head + d) % N_HEAD}, device_id_type=MESH)

    loads = {}
    for i, (name, source, target) in enumerate(
        (
            ("step", step_hbm, step_ref),
            ("decay", decay_hbm, decay_ref),
            ("seg", seg_hbm, seg_ref),
            ("in", in_hbm, in_ref),
            ("x", x_hbm, x_ref),
            ("k", k_hbm, k_ref),
            ("v", v_hbm, v_ref),
            ("out", out_hbm, out_ref),
            ("skip", skip_hbm, skip_ref),
            ("q", q_hbm, q_ref),
            ("gate", gate_hbm, gate_ref),
            ("gain", gain_hbm, gain_ref),
        )
    ):
        loads[name] = pltpu.make_async_copy(source, target, load_sem.at[i])
        loads[name].start()

    def loaded(*names):
        for name in names:
            loads[name].wait()

    def kv_copies(hop):
        return [
            pltpu.make_async_remote_copy(
                src_ref=source,
                dst_ref=target,
                send_sem=kv_send.at[hop, i],
                recv_sem=kv_recv.at[hop, i],
                device_id={"seq": succ},
                device_id_type=MESH,
            )
            for i, (source, target) in enumerate(
                (
                    (kt_buf.at[hop, pl.ds(0, HEAD_D)], kt_buf.at[hop + 1, pl.ds(0, HEAD_D)]),
                    (v_buf.at[hop], v_buf.at[hop + 1]),
                    (tag_buf.at[hop], tag_buf.at[hop + 1]),
                )
            )
        ]

    def scan_copy(d):
        return pltpu.make_async_remote_copy(
            src_ref=send_buf.at[(z + d) % RING],
            dst_ref=scan_buf.at[z],
            send_sem=a_send.at[d],
            recv_sem=a_recv.at[d],
            device_id={"seq": ring(d)},
            device_id_type=MESH,
        )

    def back_copy(d):
        return pltpu.make_async_remote_copy(
            src_ref=back_buf.at[(z + d) % RING],
            dst_ref=in_buf.at[z],
            send_sem=b_send.at[d],
            recv_sem=b_recv.at[d],
            device_id={"seq": ring(d)},
            device_id_type=MESH,
        )

    def square_copy(d):
        return pltpu.make_async_remote_copy(
            src_ref=sq_buf.at[head],
            dst_ref=sq_buf.at[head],
            send_sem=s_send.at[d],
            recv_sem=s_recv.at[d],
            device_id={"head": (head + d) % N_HEAD},
            device_id_type=MESH,
        )

    def note_copy(d):
        return pltpu.make_async_remote_copy(
            src_ref=note_buf.at[z],
            dst_ref=note_buf.at[z],
            send_sem=n_send.at[d],
            recv_sem=n_recv.at[d],
            device_id={"seq": ring(d)},
            device_id_type=MESH,
        )

    def relay_out(phase, far):
        return pltpu.make_async_remote_copy(
            src_ref=(send_buf, back_buf)[phase].at[(z + far) % RING],
            dst_ref=relay_buf.at[phase, far - 7],
            send_sem=r_send.at[phase, far - 7],
            recv_sem=r_recv.at[phase, far - 7],
            device_id={"seq": ring(RING - RING // 4)},
            device_id_type=MESH,
        )

    def relay_on(phase, far):
        return pltpu.make_async_remote_copy(
            src_ref=relay_buf.at[phase, far - 7],
            dst_ref=(scan_buf, in_buf)[phase].at[(z + RING // 4) % RING],
            send_sem=f_send.at[phase, far - 7],
            recv_sem=(a_recv, b_recv)[phase].at[far],
            device_id={"seq": ring(far + RING // 4)},
            device_id_type=MESH,
        )

    def relay(phase):
        for far in RELAYED[phase]:
            relay_out(phase, far).wait_recv()
            relay_on(phase, far).start()

    carry_copy = pltpu.make_async_remote_copy(
        src_ref=carry_buf.at[0],
        dst_ref=carry_buf.at[1],
        send_sem=c_send.at[0],
        recv_sem=c_recv.at[0],
        device_id={"seq": below},
        device_id_type=MESH,
    )
    direct = [
        sorted((d for d in range(1, RING) if d not in RELAYED[phase]), key=lambda d: -min(d, RING - d))
        for phase in range(2)
    ]

    loaded("step", "decay", "seg")
    lane = lax.broadcasted_iota(jnp.int32, (LOCAL_HEADS, TOKENS), 1)
    diagonal = lax.broadcasted_iota(jnp.int32, (LOCAL_HEADS, LOCAL_HEADS), 0) == lax.broadcasted_iota(
        jnp.int32, (LOCAL_HEADS, LOCAL_HEADS), 1
    )
    rate = jnp.sum(
        jnp.where(diagonal, jnp.broadcast_to(decay_ref[...], (LOCAL_HEADS, LOCAL_HEADS)), 0.0), axis=1, keepdims=True
    )
    cum = step_ref[...] * rate
    reach = 1
    while reach < TOKENS:
        cum = cum + jnp.where(lane >= reach, pltpu.roll(cum, reach, 1), 0.0)
        reach *= 2
    cum = cum * LOG2E
    cum_buf[...] = cum
    seg_row = seg_ref[...].astype(F32)
    seg_last = seg_row[:, TOKENS - 1 :]
    seg_first = seg_row[:, :1]
    last_cum = cum[:, TOKENS - 1 :]
    tail = jnp.where(seg_row == seg_last, jnp.exp2(jnp.minimum(cum - last_cum, 0.0)), 0.0)
    enter = jnp.where(seg_row == seg_first, jnp.exp2(-cum), 0.0)
    col_buf[...] = jnp.concatenate(
        [cum, tail, enter, jnp.zeros((128 - 3 * LOCAL_HEADS, TOKENS), F32)], axis=0
    ).T
    loaded("in", "x")
    in_map = in_ref[...]
    in_map_t = in_map.astype(F32).T.astype(BF16)
    first_half = lax.broadcasted_iota(jnp.int32, (TOKENS, 128), 1) < HEAD_P

    def pair_columns(base, p):
        a = jnp.broadcast_to(col_buf[:, base + 2 * p : base + 2 * p + 1], (TOKENS, 128))
        b = jnp.broadcast_to(col_buf[:, base + 2 * p + 1 : base + 2 * p + 2], (TOKENS, 128))
        return jnp.where(first_half, a, b)

    note_lane = lax.broadcasted_iota(jnp.int32, (1, 128), 1)
    note_buf[z] = jnp.where(
        note_lane < LOCAL_HEADS,
        jnp.exp2(-col_buf[TOKENS - 1 :, :]),
        jnp.where(note_lane == LOCAL_HEADS, seg_first, seg_last),
    )
    for p in range(PAIRS):
        weighted = (x_ref[:, p * 128 : (p + 1) * 128].astype(F32) * pair_columns(LOCAL_HEADS, p)).astype(BF16)
        end_state = dot(in_map_t, weighted).T.astype(BF16)
        for half in range(2):
            h = 2 * p + half
            send_buf[h] = end_state[half * HEAD_P : (half + 1) * HEAD_P]

    loaded("k", "v")
    kt_buf[0, :HEAD_D] = k_ref[...].astype(F32).T.astype(BF16)
    documents = lax.broadcasted_iota(jnp.int32, (16, TOKENS), 0).astype(F32)
    tag_buf[0] = seg_row

    def mask_rows(hop):
        kt_buf[hop, HEAD_D:KT_ROWS] = jnp.where(documents == tag_buf[hop], 0.0, -FAR).astype(BF16)

    mask_rows(0)
    v_buf[0] = v_ref[...]
    for hop in range(DOC_SPAN + 1):
        kt_buf[hop, KT_ROWS:] = jnp.zeros((TOKENS - KT_ROWS, TOKENS), BF16)

    pl.semaphore_wait(barrier, RING - 1 + 4 + N_HEAD - 1)
    for far in RELAYED[0]:
        relay_out(0, far).start()
    for d in direct[0]:
        scan_copy(d).start()
    for d in range(1, RING):
        note_copy(d).start()
    for copy in kv_copies(0):
        copy.start()
    scan_buf[z] = send_buf[z]

    def forward(hop):
        for copy, onward in zip(kv_copies(hop - 1), kv_copies(hop) if hop < DOC_SPAN else [None] * 3):
            copy.wait_recv()
            if onward is not None:
                onward.start()
        mask_rows(hop)

    loaded("out", "skip", "q", "gate", "gain")
    seg_col = jnp.broadcast_to(seg_row, (128, TOKENS)).T
    onehot_buf[...] = jnp.where(
        lax.broadcasted_iota(jnp.int32, (TOKENS, 128), 1).astype(F32) == seg_col, 1.0, 0.0
    ).astype(BF16)
    causal = lax.broadcasted_iota(jnp.int32, (TOKENS, TOKENS), 1) <= lax.broadcasted_iota(
        jnp.int32, (TOKENS, TOKENS), 0
    )
    same = jnp.concatenate([seg_col, seg_col], axis=1) == jnp.broadcast_to(seg_row, (TOKENS, TOKENS))
    g_buf[...] = jnp.where(causal & same, dot(out_ref[...], in_map, ((1,), (1,))), 0.0)

    def within(pairs):
        for p in pairs:
            x_pair = x_ref[:, p * 128 : (p + 1) * 128]
            zero = jnp.zeros_like(x_pair)
            total = jnp.zeros((TOKENS, 128), F32)
            for half in range(2):
                h = 2 * p + half
                gap = jnp.broadcast_to(cum_buf[h : h + 1, :], (TOKENS, TOKENS)) - jnp.broadcast_to(
                    col_buf[:, h : h + 1], (TOKENS, TOKENS)
                )
                mixing = (jnp.exp2(jnp.minimum(gap, 0.0)) * g_buf[...]).astype(BF16)
                x_half = jnp.where(first_half, x_pair, zero) if half == 0 else jnp.where(first_half, zero, x_pair)
                total = total + dot(mixing, x_half)
            skip = jnp.where(
                first_half[:1], skip_ref[:, 2 * p : 2 * p + 1], skip_ref[:, 2 * p + 1 : 2 * p + 2]
            )
            gate = gate_ref[:, p * 128 : (p + 1) * 128].astype(F32)
            opened = gate / (1.0 + jnp.exp(-gate))
            y_buf[p] = (total + skip * x_pair.astype(F32)) * opened
            enter_buf[p] = pair_columns(2 * LOCAL_HEADS, p) * opened

    def attend(hops):
        first, final = hops[0] == 0, hops[-1] == DOC_SPAN

        def one(h, _):
            columns = pl.ds(pl.multiple_of(h * HEAD_D, HEAD_D), HEAD_D)
            q = jnp.concatenate([q_ref[:, columns], onehot_buf[...]], axis=1)
            scores = []
            for hop in hops:
                s = dot(q, kt_buf[hop])
                if hop == 0:
                    s = jnp.where(causal, s, -2.0 * FAR)
                scores.append(s)
            top = scores[0]
            for s in scores[1:]:
                top = jnp.maximum(top, s)
            best = jnp.broadcast_to(jnp.max(top, axis=1, keepdims=True), (TOKENS, 128))
            if not first:
                before = max_buf[h]
                best = jnp.maximum(before, best)
            best2 = jnp.concatenate([best, best], axis=1)
            ones = jnp.ones((TOKENS, HEAD_D), BF16)
            total = None
            for hop, s in zip(hops, scores):
                weights = jnp.exp2((s - best2) * SCORE_SCALE).astype(BF16)
                part = dot(weights, jnp.concatenate([v_buf[hop], ones], axis=1))
                total = part if total is None else total + part
            if not first:
                shrink = jnp.exp2((before - best) * SCORE_SCALE)
                total = total + acc_buf[h] * jnp.concatenate([shrink, shrink], axis=1)
            if final:
                att_ref[:, columns] = (total[:, :HEAD_D] / total[:, HEAD_D:]).astype(BF16)
            else:
                acc_buf[h] = total
                max_buf[h] = best
            return 0

        lax.fori_loop(0, LOCAL_ATT, one, 0, unroll=4)

    notes = []

    def scan():
        for d in direct[0]:
            scan_copy(d).wait_recv()
        for far in RELAYED[0]:
            relay_on(0, far).wait_recv()
        for d in range(1, RING):
            note_copy(d).wait_recv()
        all_notes = jnp.concatenate([note_buf[i] for i in range(RING)], axis=0)
        decays = jnp.sum(
            jnp.where(lax.broadcasted_iota(jnp.int32, (RING, 128), 1) == z, all_notes, 0.0), axis=1, keepdims=True
        )
        decays = jnp.broadcast_to(decays, (RING, STATE_N))
        firsts = jnp.broadcast_to(all_notes[:, LOCAL_HEADS : LOCAL_HEADS + 1], (RING, STATE_N))
        lasts = jnp.broadcast_to(all_notes[:, LOCAL_HEADS + 1 : LOCAL_HEADS + 2], (RING, STATE_N))
        state = jnp.zeros((HEAD_P, STATE_N), F32)
        product = jnp.ones((1, STATE_N), F32)
        last_before = None
        for i in range(RING):
            block = scan_buf[i].astype(F32)
            decay, tag_first, tag_last = decays[i : i + 1], firsts[i : i + 1], lasts[i : i + 1]
            if i >= DOC_SPAN:
                back_buf[i] = jnp.where(tag_first == last_before, state, 0.0).astype(BF16)
            else:
                local_buf[i] = state
                notes.append((product, tag_first, last_before))
            kept = decay if i == 0 else jnp.where(tag_last == last_before, decay, 0.0)
            state = block + kept * state
            product = product * decay
            last_before = tag_last
        carry_buf[0, :HEAD_P] = state.astype(BF16)
        carry_buf[0, HEAD_P:] = jnp.broadcast_to(last_before, (16, STATE_N)).astype(BF16)
        carry_copy.start()

        for far in RELAYED[1]:

            @pl.when((z + far) % RING >= DOC_SPAN)
            def _(far=far):
                relay_out(1, far).start()

        for d in direct[1]:

            @pl.when((z + d) % RING >= DOC_SPAN)
            def _(d=d):
                back_copy(d).start()


    def carry():
        carry_copy.wait_recv()
        carried = carry_buf[1, :HEAD_P].astype(F32)
        carried_tag = carry_buf[1, HEAD_P:].astype(F32)[:1]
        for i, (product, tag_first, last_before) in enumerate(notes):
            if i == 0:
                full = jnp.where(tag_first == carried_tag, carried, 0.0)
            else:
                full = local_buf[i] + jnp.where(carried_tag == last_before, product, 0.0) * carried
                full = jnp.where(tag_first == last_before, full, 0.0)
            back_buf[i] = full.astype(BF16)

        for far in RELAYED[1]:

            @pl.when((z + far) % RING < DOC_SPAN)
            def _(far=far):
                relay_out(1, far).start()

        for d in direct[1]:

            @pl.when((z + d) % RING < DOC_SPAN)
            def _(d=d):
                back_copy(d).start()

        in_buf[z] = back_buf[z]

    def enter_block():
        for d in direct[1]:
            back_copy(d).wait_recv()
        for far in RELAYED[1]:
            relay_on(1, far).wait_recv()
        squares = jnp.zeros((TOKENS, 128), F32)
        for p in range(PAIRS):
            entering = jnp.concatenate([in_buf[2 * p], in_buf[2 * p + 1]], axis=0)
            incoming = dot(out_ref[...], entering, ((1,), (1,)))
            gated = y_buf[p] + enter_buf[p] * incoming
            y_buf[p] = gated
            squares = squares + gated * gated
        squares_t = squares.T
        partial = squares_t[:8]
        for i in range(1, 16):
            partial = partial + squares_t[8 * i : 8 * i + 8]
        sq_buf[head] = partial
        for d in range(1, N_HEAD):
            square_copy(d).start()

    def normalise():
        for d in range(1, N_HEAD):
            square_copy(d).wait_recv()
        total = sq_buf[0]
        for i in range(1, N_HEAD):
            total = total + sq_buf[i]
        mean = jnp.sum(total, axis=0, keepdims=True) * (1.0 / (SSD_HEADS * HEAD_P))
        scale = jnp.broadcast_to(lax.rsqrt(mean + 1e-05), (128, TOKENS)).T
        for p in range(PAIRS):
            state_ref[:, p * 128 : (p + 1) * 128] = (
                y_buf[p] * scale * gain_ref[:, p * 128 : (p + 1) * 128]
            ).astype(BF16)


    forward(1)
    relay(0)
    within(range(0, 8))
    forward(2)
    attend((0, 1))
    scan()
    forward(3)
    carry()
    forward(4)
    relay(1)
    attend((2, 3))
    forward(5)
    attend((4, 5))
    forward(6)
    enter_block()
    forward(7)
    attend((6, 7))
    forward(8)
    attend((8,))
    normalise()

    for hop in range(DOC_SPAN):
        for copy in kv_copies(hop):
            copy.wait_send()
    for d in direct[0]:
        scan_copy(d).wait_send()
    for d in direct[1]:
        back_copy(d).wait_send()
    for d in range(1, N_HEAD):
        square_copy(d).wait_send()
    carry_copy.wait_send()
    for phase in range(2):
        for far in RELAYED[phase]:
            relay_out(phase, far).wait_send()
            relay_on(phase, far).wait_send()
    for d in range(1, RING):
        note_copy(d).wait_send()


def per_device(mixer_input, gate_input, input_map, output_map, step_size, decay_rate, skip_gain, norm_gain, queries, key_rows, values, segment):
    width = mixer_input.shape[1]
    vmem = pl.BlockSpec(memory_space=pltpu.VMEM)
    dma = pltpu.SemaphoreType.DMA
    out = jax.ShapeDtypeStruct((TOKENS, width), BF16)
    operands = (
        mixer_input,
        gate_input,
        input_map,
        output_map,
        step_size,
        decay_rate[None, :],
        skip_gain[None, :],
        norm_gain[None, :],
        queries,
        key_rows,
        values,
        segment[None, :],
    )
    return pl.pallas_call(
        kernel,
        out_shape=(out, out),
        in_specs=[pl.BlockSpec(memory_space=pl.ANY)] * 12,
        out_specs=(vmem, vmem),
        scratch_shapes=[
            *(pltpu.VMEM(a.shape, a.dtype) for a in operands),
            dma((len(operands),)),
            pltpu.VMEM((DOC_SPAN + 1, TOKENS, TOKENS), BF16),
            pltpu.VMEM((DOC_SPAN + 1, TOKENS, HEAD_D), BF16),
            pltpu.VMEM((DOC_SPAN + 1, 1, TOKENS), F32),
            pltpu.VMEM((LOCAL_HEADS, HEAD_P, STATE_N), BF16),
            pltpu.VMEM((RING, HEAD_P, STATE_N), BF16),
            pltpu.VMEM((RING, 1, 128), F32),
            pltpu.VMEM((2, 2, HEAD_P, STATE_N), BF16),
            pltpu.VMEM((DOC_SPAN, HEAD_P, STATE_N), F32),
            pltpu.VMEM((RING, HEAD_P, STATE_N), BF16),
            pltpu.VMEM((2, MSG, STATE_N), BF16),
            pltpu.VMEM((LOCAL_HEADS, HEAD_P, STATE_N), BF16),
            pltpu.VMEM((N_HEAD, 8, TOKENS), F32),
            pltpu.VMEM((PAIRS, TOKENS, 128), F32),
            pltpu.VMEM((PAIRS, TOKENS, 128), F32),
            pltpu.VMEM((LOCAL_ATT, TOKENS, 2 * HEAD_D), F32),
            pltpu.VMEM((LOCAL_ATT, TOKENS, 128), F32),
            pltpu.VMEM((TOKENS, TOKENS), F32),
            pltpu.VMEM((TOKENS, 128), BF16),
            pltpu.VMEM((TOKENS, 128), F32),
            pltpu.VMEM((LOCAL_HEADS, TOKENS), F32),
            dma((DOC_SPAN, 3)),
            dma((DOC_SPAN, 3)),
            dma((RING,)),
            dma((RING,)),
            dma((2, 2)),
            dma((2, 2)),
            dma((2, 2)),
            dma((RING,)),
            dma((RING,)),
            dma((1,)),
            dma((1,)),
            dma((RING,)),
            dma((RING,)),
            dma((N_HEAD,)),
            dma((N_HEAD,)),
        ],
        compiler_params=pltpu.CompilerParams(collective_id=0, has_side_effects=True, vmem_limit_bytes=56 * 2**20),
        cost_estimate=pl.CostEstimate(flops=3 * 10**9, bytes_accessed=4 * 10**6, transcendentals=6 * 10**6),
    )(*operands)


def solution(mesh):
    in_specs = (
        P("seq", "head"),
        P("seq", "head"),
        P("seq", "head"),
        P("seq", "head"),
        P("head", "seq"),
        P("head"),
        P("head"),
        P("head"),
        P("seq", "head"),
        P("seq", "head"),
        P("seq", "head"),
        P("seq"),
    )
    out_specs = (P("seq", "head"), P("seq", "head"))
    return jax.shard_map(per_device, mesh=mesh, in_specs=in_specs, out_specs=out_specs, check_vma=False)
```

```python
import math

import jax
import jax.numpy as jnp
from jax import lax
from jax.experimental import pallas as pl
from jax.experimental.pallas import tpu as pltpu
from jax.sharding import PartitionSpec as P

SSD_HEADS = 128
HEAD_P = 64
STATE_N = 128
ATT_HEADS = 64
HEAD_D = 128
DOC_SPAN = 8
TOKENS = 256
N_SEQ = 64
RING = 16
RELAYED = ((7, 8), (7, 8))
N_HEAD = 8
LOCAL_HEADS = SSD_HEADS // N_HEAD
LOCAL_ATT = ATT_HEADS // N_HEAD
PAIRS = LOCAL_HEADS // 2
KT_ROWS = HEAD_D + 16
MSG = HEAD_P + 16
LOG2E = 1.0 / math.log(2.0)
SCORE_SCALE = LOG2E / math.sqrt(HEAD_D)
FAR = float(2**19)
MESH = pl.DeviceIdType.MESH
F32 = jnp.float32
BF16 = jnp.bfloat16


def dot(a, b, contract=((1,), (0,))):
    return lax.dot_general(a, b, (contract, ((), ())), preferred_element_type=F32)


def kernel(
    x_hbm, gate_hbm, in_hbm, out_hbm, step_hbm, decay_hbm, skip_hbm, gain_hbm, q_hbm, k_hbm, v_hbm, seg_hbm,
    state_ref, att_ref,
    x_ref, gate_ref, in_ref, out_ref, step_ref, decay_ref, skip_ref, gain_ref, q_ref, k_ref, v_ref, seg_ref, load_sem,
    kt_buf, v_buf, tag_buf, send_buf, scan_buf, note_buf, relay_buf, local_buf, back_buf, carry_buf, in_buf, sq_buf,
    y_buf, enter_buf, acc_buf, max_buf, g_buf, onehot_buf, col_buf, cum_buf,
    kv_send, kv_recv, n_send, n_recv, r_send, r_recv, f_send, a_send, a_recv, c_send, c_recv, b_send, b_recv, s_send, s_recv,
):
    me = lax.axis_index("seq")
    head = lax.axis_index("head")
    row, z = me // RING, me % RING
    succ, pred = (me + 1) % N_SEQ, (me + N_SEQ - 1) % N_SEQ
    below, above = (me + RING) % N_SEQ, (me + N_SEQ - RING) % N_SEQ

    def ring(d):
        return row * RING + (z + d) % RING

    barrier = pltpu.get_barrier_semaphore()
    for d in sorted(range(1, RING), key=lambda d: -min(d, RING - d)):
        pl.semaphore_signal(barrier, inc=1, device_id={"seq": ring(d)}, device_id_type=MESH)
    for other in (below, above, succ, pred):
        pl.semaphore_signal(barrier, inc=1, device_id={"seq": other}, device_id_type=MESH)
    for d in range(1, N_HEAD):
        pl.semaphore_signal(barrier, inc=1, device_id={"head": (head + d) % N_HEAD}, device_id_type=MESH)

    loads = {}
    for i, (name, source, target) in enumerate(
        (
            ("step", step_hbm, step_ref),
            ("decay", decay_hbm, decay_ref),
            ("seg", seg_hbm, seg_ref),
            ("in", in_hbm, in_ref),
            ("x", x_hbm, x_ref),
            ("k", k_hbm, k_ref),
            ("v", v_hbm, v_ref),
            ("out", out_hbm, out_ref),
            ("skip", skip_hbm, skip_ref),
            ("q", q_hbm, q_ref),
            ("gate", gate_hbm, gate_ref),
            ("gain", gain_hbm, gain_ref),
        )
    ):
        loads[name] = pltpu.make_async_copy(source, target, load_sem.at[i])
        loads[name].start()

    def loaded(*names):
        for name in names:
            loads[name].wait()

    def kv_copies(hop):
        return [
            pltpu.make_async_remote_copy(
                src_ref=source,
                dst_ref=target,
                send_sem=kv_send.at[hop, i],
                recv_sem=kv_recv.at[hop, i],
                device_id={"seq": succ},
                device_id_type=MESH,
            )
            for i, (source, target) in enumerate(
                (
                    (kt_buf.at[hop, pl.ds(0, HEAD_D)], kt_buf.at[hop + 1, pl.ds(0, HEAD_D)]),
                    (v_buf.at[hop], v_buf.at[hop + 1]),
                    (tag_buf.at[hop], tag_buf.at[hop + 1]),
                )
            )
        ]

    def scan_copy(d):
        return pltpu.make_async_remote_copy(
            src_ref=send_buf.at[(z + d) % RING],
            dst_ref=scan_buf.at[z],
            send_sem=a_send.at[d],
            recv_sem=a_recv.at[d],
            device_id={"seq": ring(d)},
            device_id_type=MESH,
        )

    def back_copy(d):
        return pltpu.make_async_remote_copy(
            src_ref=back_buf.at[(z + d) % RING],
            dst_ref=in_buf.at[z],
            send_sem=b_send.at[d],
            recv_sem=b_recv.at[d],
            device_id={"seq": ring(d)},
            device_id_type=MESH,
        )

    def square_copy(d):
        return pltpu.make_async_remote_copy(
            src_ref=sq_buf.at[head],
            dst_ref=sq_buf.at[head],
            send_sem=s_send.at[d],
            recv_sem=s_recv.at[d],
            device_id={"head": (head + d) % N_HEAD},
            device_id_type=MESH,
        )

    def note_copy(d):
        return pltpu.make_async_remote_copy(
            src_ref=note_buf.at[z],
            dst_ref=note_buf.at[z],
            send_sem=n_send.at[d],
            recv_sem=n_recv.at[d],
            device_id={"seq": ring(d)},
            device_id_type=MESH,
        )

    def relay_out(phase, far):
        return pltpu.make_async_remote_copy(
            src_ref=(send_buf, back_buf)[phase].at[(z + far) % RING],
            dst_ref=relay_buf.at[phase, far - 7],
            send_sem=r_send.at[phase, far - 7],
            recv_sem=r_recv.at[phase, far - 7],
            device_id={"seq": ring(RING - RING // 4)},
            device_id_type=MESH,
        )

    def relay_on(phase, far):
        return pltpu.make_async_remote_copy(
            src_ref=relay_buf.at[phase, far - 7],
            dst_ref=(scan_buf, in_buf)[phase].at[(z + RING // 4) % RING],
            send_sem=f_send.at[phase, far - 7],
            recv_sem=(a_recv, b_recv)[phase].at[far],
            device_id={"seq": ring(far + RING // 4)},
            device_id_type=MESH,
        )

    def relay(phase):
        for far in RELAYED[phase]:
            relay_out(phase, far).wait_recv()
            relay_on(phase, far).start()

    carry_copy = pltpu.make_async_remote_copy(
        src_ref=carry_buf.at[0],
        dst_ref=carry_buf.at[1],
        send_sem=c_send.at[0],
        recv_sem=c_recv.at[0],
        device_id={"seq": below},
        device_id_type=MESH,
    )
    direct = [
        sorted((d for d in range(1, RING) if d not in RELAYED[phase]), key=lambda d: -min(d, RING - d))
        for phase in range(2)
    ]

    loaded("step", "decay", "seg")
    lane = lax.broadcasted_iota(jnp.int32, (LOCAL_HEADS, TOKENS), 1)
    diagonal = lax.broadcasted_iota(jnp.int32, (LOCAL_HEADS, LOCAL_HEADS), 0) == lax.broadcasted_iota(
        jnp.int32, (LOCAL_HEADS, LOCAL_HEADS), 1
    )
    rate = jnp.sum(
        jnp.where(diagonal, jnp.broadcast_to(decay_ref[...], (LOCAL_HEADS, LOCAL_HEADS)), 0.0), axis=1, keepdims=True
    )
    cum = step_ref[...] * rate
    reach = 1
    while reach < TOKENS:
        cum = cum + jnp.where(lane >= reach, pltpu.roll(cum, reach, 1), 0.0)
        reach *= 2
    cum = cum * LOG2E
    cum_buf[...] = cum
    seg_row = seg_ref[...].astype(F32)
    seg_last = seg_row[:, TOKENS - 1 :]
    seg_first = seg_row[:, :1]
    last_cum = cum[:, TOKENS - 1 :]
    tail = jnp.where(seg_row == seg_last, jnp.exp2(jnp.minimum(cum - last_cum, 0.0)), 0.0)
    enter = jnp.where(seg_row == seg_first, jnp.exp2(-cum), 0.0)
    col_buf[...] = jnp.concatenate(
        [cum, tail, enter, jnp.zeros((128 - 3 * LOCAL_HEADS, TOKENS), F32)], axis=0
    ).T
    loaded("in", "x")
    in_map = in_ref[...]
    in_map_t = in_map.astype(F32).T.astype(BF16)
    first_half = lax.broadcasted_iota(jnp.int32, (TOKENS, 128), 1) < HEAD_P

    def pair_columns(base, p):
        a = jnp.broadcast_to(col_buf[:, base + 2 * p : base + 2 * p + 1], (TOKENS, 128))
        b = jnp.broadcast_to(col_buf[:, base + 2 * p + 1 : base + 2 * p + 2], (TOKENS, 128))
        return jnp.where(first_half, a, b)

    note_lane = lax.broadcasted_iota(jnp.int32, (1, 128), 1)
    note_buf[z] = jnp.where(
        note_lane < LOCAL_HEADS,
        jnp.exp2(-col_buf[TOKENS - 1 :, :]),
        jnp.where(note_lane == LOCAL_HEADS, seg_first, seg_last),
    )
    for p in range(PAIRS):
        weighted = (x_ref[:, p * 128 : (p + 1) * 128].astype(F32) * pair_columns(LOCAL_HEADS, p)).astype(BF16)
        end_state = dot(in_map_t, weighted).T.astype(BF16)
        for half in range(2):
            h = 2 * p + half
            send_buf[h] = end_state[half * HEAD_P : (half + 1) * HEAD_P]

    loaded("k", "v")
    kt_buf[0, :HEAD_D] = k_ref[...].astype(F32).T.astype(BF16)
    documents = lax.broadcasted_iota(jnp.int32, (16, TOKENS), 0).astype(F32)
    tag_buf[0] = seg_row

    def mask_rows(hop):
        kt_buf[hop, HEAD_D:KT_ROWS] = jnp.where(documents == tag_buf[hop], 0.0, -FAR).astype(BF16)

    mask_rows(0)
    v_buf[0] = v_ref[...]
    for hop in range(DOC_SPAN + 1):
        kt_buf[hop, KT_ROWS:] = jnp.zeros((TOKENS - KT_ROWS, TOKENS), BF16)

    pl.semaphore_wait(barrier, RING - 1 + 4 + N_HEAD - 1)
    for far in RELAYED[0]:
        relay_out(0, far).start()
    for d in direct[0]:
        scan_copy(d).start()
    for d in range(1, RING):
        note_copy(d).start()
    for copy in kv_copies(0):
        copy.start()
    scan_buf[z] = send_buf[z]

    def forward(hop):
        for copy, onward in zip(kv_copies(hop - 1), kv_copies(hop) if hop < DOC_SPAN else [None] * 3):
            copy.wait_recv()
            if onward is not None:
                onward.start()
        mask_rows(hop)

    loaded("out", "skip", "q", "gate", "gain")
    seg_col = jnp.broadcast_to(seg_row, (128, TOKENS)).T
    onehot_buf[...] = jnp.where(
        lax.broadcasted_iota(jnp.int32, (TOKENS, 128), 1).astype(F32) == seg_col, 1.0, 0.0
    ).astype(BF16)
    causal = lax.broadcasted_iota(jnp.int32, (TOKENS, TOKENS), 1) <= lax.broadcasted_iota(
        jnp.int32, (TOKENS, TOKENS), 0
    )
    same = jnp.concatenate([seg_col, seg_col], axis=1) == jnp.broadcast_to(seg_row, (TOKENS, TOKENS))
    g_buf[...] = jnp.where(causal & same, dot(out_ref[...], in_map, ((1,), (1,))), 0.0)

    def within(pairs):
        for p in pairs:
            x_pair = x_ref[:, p * 128 : (p + 1) * 128]
            zero = jnp.zeros_like(x_pair)
            total = jnp.zeros((TOKENS, 128), F32)
            for half in range(2):
                h = 2 * p + half
                gap = jnp.broadcast_to(cum_buf[h : h + 1, :], (TOKENS, TOKENS)) - jnp.broadcast_to(
                    col_buf[:, h : h + 1], (TOKENS, TOKENS)
                )
                mixing = (jnp.exp2(jnp.minimum(gap, 0.0)) * g_buf[...]).astype(BF16)
                x_half = jnp.where(first_half, x_pair, zero) if half == 0 else jnp.where(first_half, zero, x_pair)
                total = total + dot(mixing, x_half)
            skip = jnp.where(
                first_half[:1], skip_ref[:, 2 * p : 2 * p + 1], skip_ref[:, 2 * p + 1 : 2 * p + 2]
            )
            gate = gate_ref[:, p * 128 : (p + 1) * 128].astype(F32)
            opened = gate / (1.0 + jnp.exp(-gate))
            y_buf[p] = (total + skip * x_pair.astype(F32)) * opened
            enter_buf[p] = pair_columns(2 * LOCAL_HEADS, p) * opened

    def attend(hops):
        first, final = hops[0] == 0, hops[-1] == DOC_SPAN

        def one(h, _):
            columns = pl.ds(pl.multiple_of(h * HEAD_D, HEAD_D), HEAD_D)
            q = jnp.concatenate([q_ref[:, columns], onehot_buf[...]], axis=1)
            scores = []
            for hop in hops:
                s = dot(q, kt_buf[hop])
                if hop == 0:
                    s = jnp.where(causal, s, -2.0 * FAR)
                scores.append(s)
            top = scores[0]
            for s in scores[1:]:
                top = jnp.maximum(top, s)
            best = jnp.broadcast_to(jnp.max(top, axis=1, keepdims=True), (TOKENS, 128))
            if not first:
                before = max_buf[h]
                best = jnp.maximum(before, best)
            best2 = jnp.concatenate([best, best], axis=1)
            ones = jnp.ones((TOKENS, HEAD_D), BF16)
            total = None
            for hop, s in zip(hops, scores):
                weights = jnp.exp2((s - best2) * SCORE_SCALE).astype(BF16)
                part = dot(weights, jnp.concatenate([v_buf[hop], ones], axis=1))
                total = part if total is None else total + part
            if not first:
                shrink = jnp.exp2((before - best) * SCORE_SCALE)
                total = total + acc_buf[h] * jnp.concatenate([shrink, shrink], axis=1)
            if final:
                att_ref[:, columns] = (total[:, :HEAD_D] / total[:, HEAD_D:]).astype(BF16)
            else:
                acc_buf[h] = total
                max_buf[h] = best
            return 0

        lax.fori_loop(0, LOCAL_ATT, one, 0, unroll=8)

    notes = []

    def scan():
        for d in direct[0]:
            scan_copy(d).wait_recv()
        for far in RELAYED[0]:
            relay_on(0, far).wait_recv()
        for d in range(1, RING):
            note_copy(d).wait_recv()
        all_notes = jnp.concatenate([note_buf[i] for i in range(RING)], axis=0)
        decays = jnp.sum(
            jnp.where(lax.broadcasted_iota(jnp.int32, (RING, 128), 1) == z, all_notes, 0.0), axis=1, keepdims=True
        )
        decays = jnp.broadcast_to(decays, (RING, STATE_N))
        firsts = jnp.broadcast_to(all_notes[:, LOCAL_HEADS : LOCAL_HEADS + 1], (RING, STATE_N))
        lasts = jnp.broadcast_to(all_notes[:, LOCAL_HEADS + 1 : LOCAL_HEADS + 2], (RING, STATE_N))
        state = jnp.zeros((HEAD_P, STATE_N), F32)
        product = jnp.ones((1, STATE_N), F32)
        last_before = None
        for i in range(RING):
            block = scan_buf[i].astype(F32)
            decay, tag_first, tag_last = decays[i : i + 1], firsts[i : i + 1], lasts[i : i + 1]
            if i >= DOC_SPAN:
                back_buf[i] = jnp.where(tag_first == last_before, state, 0.0).astype(BF16)
            else:
                local_buf[i] = state
                notes.append((product, tag_first, last_before))
            kept = decay if i == 0 else jnp.where(tag_last == last_before, decay, 0.0)
            state = block + kept * state
            product = product * decay
            last_before = tag_last
        carry_buf[0, :HEAD_P] = state.astype(BF16)
        carry_buf[0, HEAD_P:] = jnp.broadcast_to(last_before, (16, STATE_N)).astype(BF16)
        carry_copy.start()

        for far in RELAYED[1]:

            @pl.when((z + far) % RING >= DOC_SPAN)
            def _(far=far):
                relay_out(1, far).start()

        for d in direct[1]:

            @pl.when((z + d) % RING >= DOC_SPAN)
            def _(d=d):
                back_copy(d).start()


    def carry():
        carry_copy.wait_recv()
        carried = carry_buf[1, :HEAD_P].astype(F32)
        carried_tag = carry_buf[1, HEAD_P:].astype(F32)[:1]
        for i, (product, tag_first, last_before) in enumerate(notes):
            if i == 0:
                full = jnp.where(tag_first == carried_tag, carried, 0.0)
            else:
                full = local_buf[i] + jnp.where(carried_tag == last_before, product, 0.0) * carried
                full = jnp.where(tag_first == last_before, full, 0.0)
            back_buf[i] = full.astype(BF16)

        for far in RELAYED[1]:

            @pl.when((z + far) % RING < DOC_SPAN)
            def _(far=far):
                relay_out(1, far).start()

        for d in direct[1]:

            @pl.when((z + d) % RING < DOC_SPAN)
            def _(d=d):
                back_copy(d).start()

        in_buf[z] = back_buf[z]

    def enter_block():
        for d in direct[1]:
            back_copy(d).wait_recv()
        for far in RELAYED[1]:
            relay_on(1, far).wait_recv()
        squares = jnp.zeros((TOKENS, 128), F32)
        for p in range(PAIRS):
            entering = jnp.concatenate([in_buf[2 * p], in_buf[2 * p + 1]], axis=0)
            incoming = dot(out_ref[...], entering, ((1,), (1,)))
            gated = y_buf[p] + enter_buf[p] * incoming
            y_buf[p] = gated
            squares = squares + gated * gated
        squares_t = squares.T
        partial = squares_t[:8]
        for i in range(1, 16):
            partial = partial + squares_t[8 * i : 8 * i + 8]
        sq_buf[head] = partial
        for d in range(1, N_HEAD):
            square_copy(d).start()

    def normalise():
        for d in range(1, N_HEAD):
            square_copy(d).wait_recv()
        total = sq_buf[0]
        for i in range(1, N_HEAD):
            total = total + sq_buf[i]
        mean = jnp.sum(total, axis=0, keepdims=True) * (1.0 / (SSD_HEADS * HEAD_P))
        scale = jnp.broadcast_to(lax.rsqrt(mean + 1e-05), (128, TOKENS)).T
        for p in range(PAIRS):
            state_ref[:, p * 128 : (p + 1) * 128] = (
                y_buf[p] * scale * gain_ref[:, p * 128 : (p + 1) * 128]
            ).astype(BF16)


    forward(1)
    relay(0)
    within(range(0, 8))
    forward(2)
    attend((0, 1))
    scan()
    forward(3)
    carry()
    forward(4)
    relay(1)
    attend((2, 3))
    forward(5)
    attend((4, 5))
    forward(6)
    enter_block()
    forward(7)
    attend((6, 7))
    forward(8)
    attend((8,))
    normalise()

    for hop in range(DOC_SPAN):
        for copy in kv_copies(hop):
            copy.wait_send()
    for d in direct[0]:
        scan_copy(d).wait_send()
    for d in direct[1]:
        back_copy(d).wait_send()
    for d in range(1, N_HEAD):
        square_copy(d).wait_send()
    carry_copy.wait_send()
    for phase in range(2):
        for far in RELAYED[phase]:
            relay_out(phase, far).wait_send()
            relay_on(phase, far).wait_send()
    for d in range(1, RING):
        note_copy(d).wait_send()


def per_device(mixer_input, gate_input, input_map, output_map, step_size, decay_rate, skip_gain, norm_gain, queries, key_rows, values, segment):
    width = mixer_input.shape[1]
    vmem = pl.BlockSpec(memory_space=pltpu.VMEM)
    dma = pltpu.SemaphoreType.DMA
    out = jax.ShapeDtypeStruct((TOKENS, width), BF16)
    operands = (
        mixer_input,
        gate_input,
        input_map,
        output_map,
        step_size,
        decay_rate[None, :],
        skip_gain[None, :],
        norm_gain[None, :],
        queries,
        key_rows,
        values,
        segment[None, :],
    )
    return pl.pallas_call(
        kernel,
        out_shape=(out, out),
        in_specs=[pl.BlockSpec(memory_space=pl.ANY)] * 12,
        out_specs=(vmem, vmem),
        scratch_shapes=[
            *(pltpu.VMEM(a.shape, a.dtype) for a in operands),
            dma((len(operands),)),
            pltpu.VMEM((DOC_SPAN + 1, TOKENS, TOKENS), BF16),
            pltpu.VMEM((DOC_SPAN + 1, TOKENS, HEAD_D), BF16),
            pltpu.VMEM((DOC_SPAN + 1, 1, TOKENS), F32),
            pltpu.VMEM((LOCAL_HEADS, HEAD_P, STATE_N), BF16),
            pltpu.VMEM((RING, HEAD_P, STATE_N), BF16),
            pltpu.VMEM((RING, 1, 128), F32),
            pltpu.VMEM((2, 2, HEAD_P, STATE_N), BF16),
            pltpu.VMEM((DOC_SPAN, HEAD_P, STATE_N), F32),
            pltpu.VMEM((RING, HEAD_P, STATE_N), BF16),
            pltpu.VMEM((2, MSG, STATE_N), BF16),
            pltpu.VMEM((LOCAL_HEADS, HEAD_P, STATE_N), BF16),
            pltpu.VMEM((N_HEAD, 8, TOKENS), F32),
            pltpu.VMEM((PAIRS, TOKENS, 128), F32),
            pltpu.VMEM((PAIRS, TOKENS, 128), F32),
            pltpu.VMEM((LOCAL_ATT, TOKENS, 2 * HEAD_D), F32),
            pltpu.VMEM((LOCAL_ATT, TOKENS, 128), F32),
            pltpu.VMEM((TOKENS, TOKENS), F32),
            pltpu.VMEM((TOKENS, 128), BF16),
            pltpu.VMEM((TOKENS, 128), F32),
            pltpu.VMEM((LOCAL_HEADS, TOKENS), F32),
            dma((DOC_SPAN, 3)),
            dma((DOC_SPAN, 3)),
            dma((RING,)),
            dma((RING,)),
            dma((2, 2)),
            dma((2, 2)),
            dma((2, 2)),
            dma((RING,)),
            dma((RING,)),
            dma((1,)),
            dma((1,)),
            dma((RING,)),
            dma((RING,)),
            dma((N_HEAD,)),
            dma((N_HEAD,)),
        ],
        compiler_params=pltpu.CompilerParams(collective_id=0, has_side_effects=True, vmem_limit_bytes=56 * 2**20),
        cost_estimate=pl.CostEstimate(flops=3 * 10**9, bytes_accessed=4 * 10**6, transcendentals=6 * 10**6),
    )(*operands)


def solution(mesh):
    in_specs = (
        P("seq", "head"),
        P("seq", "head"),
        P("seq", "head"),
        P("seq", "head"),
        P("head", "seq"),
        P("head"),
        P("head"),
        P("head"),
        P("seq", "head"),
        P("seq", "head"),
        P("seq", "head"),
        P("seq"),
    )
    out_specs = (P("seq", "head"), P("seq", "head"))
    return jax.shard_map(per_device, mesh=mesh, in_specs=in_specs, out_specs=out_specs, check_vma=False)
```
